256 devices in a mesh: pair: 128 (over y, z, x_hi, core), vir: 2 (over x_lo).
Axes of the slice: x: 4 (x_hi: 2, x_lo: 2; x = x_hi * 2 + x_lo), y: 4, z: 8, core: 2. Of those that a mesh axis runs over, the one named last changes fastest.
Arguments:
- amplitudes: bfloat16 [2, 768, 256, 256], P(None, 'pair', None, 'vir'), may hold values from -24 to 24
- integrals: bfloat16 [2, 4, 24, 256, 256], P(None, None, None, 'vir'), may hold values from -0.0546875 to 0.0546875
- pair_table: int32 [768], replicated, may hold values from 0 to 767, each once
- kramers: int32 [256], replicated, may hold values from 0 to 255, each once
Outputs:
- residual: bfloat16 [2, 4, 32, 256, 256], P(None, None, None, 'pair', 'vir')
The draws below stay inside these ranges and needn't reach their ends.
Inputs may be any that keep to these rules, and one draw needn't show every extreme that they name: `pair_table`: a permutation: every occupied pair stands in exactly one slot. `kramers`: a permutation of the virtual spinors.
All inputs are finite; a program needn't handle non-finite values.
Results may differ from the reference program's by a relative error of at most 0.00105.
Values may be sent and summed in bfloat16 or wider, within the bound.
No kernel may reach another device: no remote copies, remote signals or barrier semaphores. Data moves between devices by JAX's collectives and lax.ppermute only.
A program may use at most 128 MiB of HBM per device.

```python
import jax
import jax.numpy as jnp

O = 32
KW = 24
V = 256
JW = 4
NP = 768


def strengthened(values, key, source, target, shards_of, factor):
    def block_of(dim):
        return (jnp.arange(values.shape[dim]) // (values.shape[dim] // shards_of)).reshape((-1,) + (1,) * (values.ndim - 1 - dim))

    first = jax.random.permutation(key, shards_of)[block_of(target)]
    other_side = (block_of(target) + shards_of // 2) % shards_of
    return jnp.where((block_of(source) == first) | (block_of(source) == other_side), factor * values, values)


def shard_levels(rng, extent, split, smallest, top_value):
    def one(axis_at, blocks):
        steps = jax.random.uniform(jax.random.fold_in(jax.random.fold_in(rng, 6), axis_at), (blocks,), jnp.float32, smallest / len(split), top_value / len(split))
        return jnp.repeat(jnp.exp(steps), extent[axis_at] // blocks).reshape((-1,) + (1,) * (len(extent) - axis_at - 1))

    level = one(*split[0])
    for cut in split[1:]:
        level = level * one(*cut)
    return level


def normal_values(rng, dims, width, bound, cuts=(), held_as=jnp.bfloat16):
    gain = shard_levels(rng, dims, cuts, -0.22, 0.18) if cuts else 1.0
    array = jax.random.normal(rng, dims, jnp.float32) * width * gain
    return jnp.minimum(jnp.maximum(array, -bound), bound).astype(held_as)


def noise_with(stream_key, shape, spread, most, pieces, heavy, held_as=jnp.bfloat16):
    result = spread * jax.random.normal(stream_key, shape, jnp.float32)
    if pieces:
        result = result * shard_levels(stream_key, shape, pieces, -0.22, 0.18)
    return jnp.clip(strengthened(result, jax.random.fold_in(stream_key, 3), *heavy), -most, most).astype(held_as)


def setup_inputs(seed: int = 0) -> dict:
    splits = jax.random.split(jax.random.key(seed), 5)
    return {
        "amplitudes": noise_with(splits[0], (2, NP, V, V), 1.0, 24.0, ((1, 128), (3, 2)), (1, 2, 128, 5.5)),
        "integrals": normal_values(splits[1], (2, JW, KW, V, V), (2 * KW * V) ** -0.5, 0.0546875, ((3, 2),)),
        "pair_table": jax.random.permutation(splits[2], NP).astype(jnp.int32),
        "kramers": jax.random.permutation(splits[3], V).astype(jnp.int32),
    }


def reference(amplitudes, integrals, pair_table, kramers):
    ordered = jnp.zeros_like(amplitudes).at[:, pair_table].set(amplitudes)
    ordered = ordered.reshape(2, O, KW, V, V)
    natural = jnp.zeros_like(integrals).at[..., kramers].set(integrals)
    rows = jnp.transpose(ordered, (0, 1, 3, 2, 4)).reshape(2, O * V, KW * V)
    blocks = []
    for window in range(JW):
        slab_matrix = natural[:, window].reshape(2, KW * V, V)
        real_part = jnp.dot(rows[0], slab_matrix[0], preferred_element_type=jnp.float32) - jnp.dot(rows[1], slab_matrix[1], preferred_element_type=jnp.float32)
        imag_part = jnp.dot(rows[0], slab_matrix[1], preferred_element_type=jnp.float32) + jnp.dot(rows[1], slab_matrix[0], preferred_element_type=jnp.float32)
        cycle = jnp.stack([real_part, imag_part]).reshape(2, O, V, V)
        blocks.append((cycle - jnp.swapaxes(cycle, 2, 3)).astype(jnp.bfloat16))
    return jnp.stack(blocks, axis=1)
```

```python
import functools

import jax
import jax.numpy as jnp
from jax import lax
from jax.experimental import pallas as pl
from jax.experimental.pallas import tpu as pltpu
from jax.sharding import Mesh
from jax.sharding import PartitionSpec as P

F32 = jnp.float32
BF16 = jnp.bfloat16
NT = (((1,), (1,)), ((), ()))
VMEM_LIMIT = 24 * 1024 * 1024
IN_VMEM = pl.BlockSpec(memory_space=pltpu.VMEM)
IN_HBM = pl.BlockSpec(memory_space=pl.ANY)
IN_SMEM = pl.BlockSpec(memory_space=pltpu.SMEM)
PARAMS = pltpu.CompilerParams(vmem_limit_bytes=VMEM_LIMIT)


def cost(flops, moved_bytes):
    return pl.CostEstimate(flops=int(flops), bytes_accessed=int(moved_bytes), transcendentals=0)


def regroup_kernel(src, dst, planes, sems):
    parts, slots = src.shape[:2]
    copies = [
        pltpu.make_async_copy(src.at[part, slot], planes.at[part, slot], sems.at[part, slot])
        for part in range(parts)
        for slot in range(slots)
    ]
    for copy in copies:
        copy.start()
    for part in range(parts):
        for slot in range(slots):
            copies[part * slots + slot].wait()
            dst[:, slot * parts + part] = planes[part, slot]


def regroup(amplitudes, chips):
    parts, slots, rows, width = amplitudes.shape
    here = rows // chips
    planes = amplitudes.reshape(parts, slots, chips, here, width)
    return pl.pallas_call(
        regroup_kernel,
        out_shape=jax.ShapeDtypeStruct((chips, parts * slots, here, width), amplitudes.dtype),
        in_specs=[IN_HBM],
        out_specs=IN_VMEM,
        scratch_shapes=[pltpu.VMEM(planes.shape, planes.dtype), pltpu.SemaphoreType.DMA((parts, slots))],
        compiler_params=PARAMS,
        name="regroup",
    )(pltpu.with_memory_space_constraint(planes, pltpu.HBM))


def slab_copies(place, turn, integrals, slabs, sems):
    vir, core = place[0] % 2, (place[0] // 2) % 2
    window = 2 * core + (1 - vir if turn == 0 else vir)
    return [pltpu.make_async_copy(integrals.at[part, window], slabs.at[part], sems.at[part]) for part in range(2)]


def spread_rows(moved, wide, slots_by):
    slots = slots_by.shape[0]
    width = moved.shape[1]
    rows = moved.shape[0] // slots
    pitch = slots + 1
    slots_a_step = 32

    def step(index, carry):
        at = index * slots_a_step
        values = moved[pl.ds(pl.multiple_of(at * rows, slots_a_step * rows), slots_a_step * rows), :].astype(F32)
        for slot in range(slots_a_step):
            wide[pl.ds(at + slot, rows, stride=pitch), :] = values[slot * rows : (slot + 1) * rows]
        return carry

    lax.fori_loop(0, slots // slots_a_step, step, 0)
    for row in range(rows):
        slots_by[:, row * width : (row + 1) * width] = wide[row * pitch : row * pitch + slots, :].astype(BF16)


def ordered_blocks(moved, chooser, wide, slots_by, occupied):
    spread_rows(moved, wide, slots_by)
    width = moved.shape[1]
    rows = slots_by.shape[1] // width
    ks_a_block = 8
    for start in range(0, chooser.shape[0] // occupied, ks_a_block):
        ordered = jnp.dot(
            chooser[start * occupied : (start + ks_a_block) * occupied, :], slots_by[...], preferred_element_type=F32
        ).astype(BF16)
        for k in range(ks_a_block):
            for row in range(rows):
                block = ordered[k * occupied : (k + 1) * occupied, row * width : (row + 1) * width]
                yield slice(row * occupied, (row + 1) * occupied), slice((start + k) * width, (start + k + 1) * width), block


def choose(chooser, table, occupied):
    pairs, slots = chooser.shape
    lanes = 128
    row = lax.broadcasted_iota(jnp.int32, (pairs, lanes), 0)
    wanted = row % occupied * (pairs // occupied) + row // occupied
    for start in range(0, slots, lanes):
        chooser[:, start : start + lanes] = (table[:, start : start + lanes] == wanted).astype(BF16)


def order_kernel(place, moved, tables, integrals, matrices, slabs, there, here, wide, slots_by, sems, *, occupied):
    copies = slab_copies(place, 0, integrals, slabs, sems)
    for copy in copies:
        copy.start()
    core = (place[0] // 2) % 2
    choose(here, tables[core], occupied)
    for at, lanes, block in ordered_blocks(moved, here, wide, slots_by, occupied):
        matrices[at, lanes] = block
    choose(there, tables[1 - core], occupied)
    for copy in copies:
        copy.wait()


def order(place, moved, tables, integrals, occupied):
    slots = tables.shape[2]
    pairs = 2 * slots
    width = moved.shape[1]
    rows = moved.shape[0] // slots
    return pl.pallas_call(
        functools.partial(order_kernel, occupied=occupied),
        out_shape=(
            pltpu.VMEM((rows * occupied, pairs // occupied * width), BF16),
            pltpu.VMEM((2,) + integrals.shape[2:], BF16),
            pltpu.VMEM((pairs, slots), BF16),
        ),
        in_specs=[IN_SMEM, IN_VMEM, IN_VMEM, IN_HBM],
        out_specs=(IN_VMEM,) * 3,
        scratch_shapes=[
            pltpu.VMEM((pairs, slots), BF16),
            pltpu.VMEM(((slots + 1) * rows, width), F32),
            pltpu.VMEM((slots, rows * width), BF16),
            pltpu.SemaphoreType.DMA((2,)),
        ],
        compiler_params=PARAMS,
        cost_estimate=cost(2 * pairs * slots * rows * width, integrals.size),
        name="order",
    )(place, moved, tables, integrals)


def product_into(out, matrices, slabs, copies=()):
    half = matrices.shape[0] // 2
    for copy in copies[:1]:
        copy.wait()
    by_real = jnp.dot(matrices[...], slabs[0], preferred_element_type=F32)
    for copy in copies[1:]:
        copy.wait()
    by_imag = jnp.dot(matrices[...], slabs[1], preferred_element_type=F32)
    out[:half] = by_real[:half] - by_imag[half:]
    out[half:] = by_real[half:] + by_imag[:half]


def first_kernel(mine, moved, chooser, slabs, matrices, out, wide, slots_by, *, occupied):
    for at, lanes, block in ordered_blocks(moved, chooser, wide, slots_by, occupied):
        matrices[at, lanes] = mine[at, lanes] + block
    product_into(out, matrices, slabs)


def first_window(mine, moved, chooser, slabs, occupied):
    width = moved.shape[1]
    slots = chooser.shape[1]
    rows = moved.shape[0] // slots
    full_virtual = slabs.shape[-1]
    return pl.pallas_call(
        functools.partial(first_kernel, occupied=occupied),
        out_shape=(
            jax.ShapeDtypeStruct(mine.shape, BF16),
            jax.ShapeDtypeStruct((mine.shape[0], full_virtual), F32),
        ),
        in_specs=[IN_VMEM] * 4,
        out_specs=(IN_VMEM,) * 2,
        scratch_shapes=[pltpu.VMEM(((slots + 1) * rows, width), F32), pltpu.VMEM((slots, rows * width), BF16)],
        compiler_params=PARAMS,
        cost_estimate=cost(4 * mine.size * full_virtual, 4 * mine.size),
        name="first_window",
    )(mine, moved, chooser, pltpu.with_memory_space_constraint(slabs, pltpu.VMEM))


def second_kernel(place, matrices, integrals, out, slabs, sems):
    vir, core = place[0] % 2, (place[0] // 2) % 2
    cuts = sems.shape[1]
    depth = slabs.shape[1] // cuts
    copies = [
        pltpu.make_async_copy(
            integrals.at[part, 2 * core + vir, pl.ds(cut * depth, depth)],
            slabs.at[part, pl.ds(cut * depth, depth)],
            sems.at[part, cut],
        )
        for part in range(2)
        for cut in range(cuts)
    ]
    copies[0].start()
    copies[1].start()
    for at, copy in enumerate(copies):
        copy.wait()
        if at + 2 < len(copies):
            copies[at + 2].start()
    product_into(out, matrices, slabs)


def second_window(place, matrices, integrals):
    depth, full_virtual = integrals.shape[2:]
    return pl.pallas_call(
        second_kernel,
        out_shape=jax.ShapeDtypeStruct((matrices.shape[0], full_virtual), F32),
        in_specs=[IN_SMEM, IN_VMEM, IN_HBM],
        out_specs=IN_VMEM,
        scratch_shapes=[pltpu.VMEM((2, depth, full_virtual), BF16), pltpu.SemaphoreType.DMA((2, 4))],
        compiler_params=PARAMS,
        cost_estimate=cost(4 * matrices.size * full_virtual, 4 * matrices.size),
        name="second_window",
    )(place, matrices, integrals)


def chosen(values, order_by):
    high = values.astype(BF16)
    rest = values - high.astype(F32)
    middle = rest.astype(BF16)
    low = (rest - middle.astype(F32)).astype(BF16)
    total = lax.dot_general(low, order_by, NT, preferred_element_type=F32)
    total += lax.dot_general(middle, order_by, NT, preferred_element_type=F32)
    return total + lax.dot_general(high, order_by, NT, preferred_element_type=F32)


def combine_kernel(kept, got, natural_order, chip_order, own, mirror):
    full_virtual = kept.shape[1]
    rows = kept.shape[0] // 2
    chips = mirror.shape[0] // 8
    here = full_virtual // chips
    occupied = rows // here
    lane = lax.broadcasted_iota(jnp.int32, (occupied, 2 * chips), 1)
    values = kept[...] + got[...]
    by_chip = chosen(values, chip_order[...])
    own[...] = chosen(values, natural_order[...])
    for part in range(2):
        for row in range(0, here, 2):
            at = part * rows + row * occupied
            blocks = []
            for other in range(0, here, 2):
                lanes = slice(other * chips, (other + 2) * chips)
                low = by_chip[at : at + occupied, lanes]
                high = by_chip[at + occupied : at + 2 * occupied, lanes]
                blocks.append(jnp.where(lane < chips, low, pltpu.roll(high, chips, 1)))
                blocks.append(jnp.where(lane < chips, pltpu.roll(low, chips, 1), high))
            turned = jnp.concatenate(blocks, axis=0).T
            mirror[pl.ds(2 * row + part, chips, stride=8), :] = turned[:chips]
            mirror[pl.ds(2 * (row + 1) + part, chips, stride=8), :] = turned[chips:]


def combine(kept, got, natural_order, chip_order, chips):
    return pl.pallas_call(
        combine_kernel,
        out_shape=(jax.ShapeDtypeStruct(kept.shape, F32), jax.ShapeDtypeStruct((chips * 8, kept.shape[0] // 2), F32)),
        compiler_params=PARAMS,
        name="combine",
    )(kept, got, natural_order, chip_order)


def subtract_kernel(place, own, mirror, keep, to_core, to_vir, to_both, block):
    vir, core = place[0] % 2, (place[0] // 2) % 2
    here = 2 * block.shape[1]
    rows, full_virtual = own.shape[0] // 2, own.shape[1]
    occupied = rows // here
    half = full_virtual // 2
    lanes = (slice(0, half), slice(half, full_virtual))
    for part in range(2):
        values = own[part * rows : (part + 1) * rows] - mirror[pl.ds(part, full_virtual, stride=2), :].T
        for row in range(here):
            for side in range(2):
                block[part, row // 2, side, pl.ds(row % 2, occupied, stride=2), :] = values[
                    row * occupied : (row + 1) * occupied, lanes[side]
                ]
    for target, to_side, to_half in (
        (keep, core, vir),
        (to_core, 1 - core, vir),
        (to_vir, core, 1 - vir),
        (to_both, 1 - core, 1 - vir),
    ):
        for part in range(2):
            target[part] = block[part, to_side, to_half].astype(BF16)


def subtract(place, own, mirror):
    rows, full_virtual = own.shape[0] // 2, own.shape[1]
    piece = jax.ShapeDtypeStruct((2, rows // 2, full_virtual // 2), BF16)
    return pl.pallas_call(
        subtract_kernel,
        out_shape=(piece,) * 4,
        in_specs=[IN_SMEM, IN_VMEM, IN_VMEM],
        out_specs=(IN_VMEM,) * 4,
        scratch_shapes=[pltpu.VMEM((2, 2, 2, rows // 2, full_virtual // 2), F32)],
        compiler_params=PARAMS,
        name="subtract",
    )(place, own, mirror)


def finish_kernel(place, keep, from_core, from_vir, from_both, out):
    vir, core = place[0] % 2, (place[0] // 2) % 2
    out[:, 2 * core + vir] = keep[...]
    out[:, 2 * (1 - core) + vir] = from_core[...]
    out[:, 2 * core + 1 - vir] = from_vir[...]
    out[:, 2 * (1 - core) + 1 - vir] = from_both[...]


def finish(place, pieces):
    _, rows, width = pieces[0].shape
    return pl.pallas_call(
        finish_kernel,
        out_shape=jax.ShapeDtypeStruct((2, 4, rows, width), BF16),
        in_specs=[IN_SMEM] + [IN_VMEM] * 4,
        out_specs=IN_VMEM,
        compiler_params=PARAMS,
        name="finish",
    )(place, *pieces)


SWAP = [(0, 1), (1, 0)]
SWAP_BOTH = [(0, 3), (1, 2), (2, 1), (3, 0)]


def body(amplitudes, integrals, pair_table, kramers):
    chips = lax.axis_size("chip")
    place = lax.axis_index(("chip", "core", "vir")).astype(jnp.int32).reshape(1)
    windows, summed_occ = integrals.shape[1:3]
    pairs = pair_table.shape[0]
    occupied = pairs // summed_occ
    slots, full_virtual, width = amplitudes.shape[1:]
    here = full_virtual // chips

    pieces = regroup(amplitudes, chips)
    moved = lax.all_to_all(pieces, "chip", split_axis=0, concat_axis=0, tiled=True)
    moved = moved.reshape(-1, width)
    flat = integrals.reshape(2, windows, summed_occ * integrals.shape[3], full_virtual)
    flat = pltpu.with_memory_space_constraint(flat, pltpu.HBM)
    across = lax.ppermute(moved, "core", SWAP)

    tables = pair_table.reshape(chips, 2, slots).transpose(1, 0, 2).reshape(2, 1, chips * slots)
    places = jnp.arange(full_virtual, dtype=jnp.int32)[:, None]
    natural_order = (kramers[None, :] == places).astype(BF16)
    chip_order = (kramers[None, :] == places % chips * here + places // chips).astype(BF16)

    mine, slabs, chooser = order(place, moved, tables, flat, occupied)
    matrices, to_send = first_window(mine, across, chooser, slabs, occupied)
    got = lax.ppermute(to_send, "vir", SWAP)
    kept = second_window(place, matrices, flat)
    own, mirror = combine(kept, got, natural_order, chip_order, chips)
    mirror = lax.all_to_all(mirror.reshape(chips, 8, -1), "chip", split_axis=0, concat_axis=0, tiled=True)
    keep, to_core, to_vir, to_both = subtract(place, own, mirror.reshape(chips * 8, -1))
    from_vir = lax.ppermute(to_vir, "vir", SWAP)
    from_both = lax.ppermute(to_both, ("core", "vir"), SWAP_BOTH)
    from_core = lax.ppermute(to_core, "core", SWAP)
    got_pieces = (keep, from_core, from_vir, from_both)
    out = finish(place, got_pieces)
    return out.reshape(2, windows, occupied, here // 2, width)


def solution(mesh):
    pair, vir = mesh.devices.shape
    split = Mesh(mesh.devices.reshape(pair // 2, 2, vir), ("chip", "core", "vir"))
    over_pair = ("chip", "core")
    placed = (P(None, over_pair, None, "vir"), P(None, None, None, "vir", None), P(), P())
    return jax.shard_map(
        body,
        mesh=split,
        in_specs=placed,
        out_specs=P(None, None, None, over_pair, "vir"),
        check_vma=False,
    )
```

```python
import functools

import jax
import jax.numpy as jnp
from jax import lax
from jax.experimental import pallas as pl
from jax.experimental.pallas import tpu as pltpu
from jax.sharding import Mesh
from jax.sharding import PartitionSpec as P

F32 = jnp.float32
BF16 = jnp.bfloat16
NT = (((1,), (1,)), ((), ()))
VMEM_LIMIT = 24 * 1024 * 1024
IN_VMEM = pl.BlockSpec(memory_space=pltpu.VMEM)
KS_A_BLOCK = 8
IN_HBM = pl.BlockSpec(memory_space=pl.ANY)
IN_SMEM = pl.BlockSpec(memory_space=pltpu.SMEM)
PARAMS = pltpu.CompilerParams(vmem_limit_bytes=VMEM_LIMIT)


def cost(flops, moved_bytes):
    return pl.CostEstimate(flops=int(flops), bytes_accessed=int(moved_bytes), transcendentals=0)


def regroup_kernel(src, dst, planes, sems):
    parts, slots = src.shape[:2]
    copies = [
        pltpu.make_async_copy(src.at[part, slot], planes.at[part, slot], sems.at[part, slot])
        for part in range(parts)
        for slot in range(slots)
    ]
    for copy in copies:
        copy.start()
    for part in range(parts):
        for slot in range(slots):
            copies[part * slots + slot].wait()
            dst[:, slot * parts + part] = planes[part, slot]


def regroup(amplitudes, chips):
    parts, slots, rows, width = amplitudes.shape
    here = rows // chips
    planes = amplitudes.reshape(parts, slots, chips, here, width)
    return pl.pallas_call(
        regroup_kernel,
        out_shape=jax.ShapeDtypeStruct((chips, parts * slots, here, width), amplitudes.dtype),
        in_specs=[IN_HBM],
        out_specs=IN_VMEM,
        scratch_shapes=[pltpu.VMEM(planes.shape, planes.dtype), pltpu.SemaphoreType.DMA((parts, slots))],
        compiler_params=PARAMS,
        name="regroup",
    )(pltpu.with_memory_space_constraint(planes, pltpu.HBM))


def slab_copies(place, turn, integrals, slabs, sems):
    vir, core = place[0] % 2, (place[0] // 2) % 2
    window = 2 * core + (1 - vir if turn == 0 else vir)
    return [pltpu.make_async_copy(integrals.at[part, window], slabs.at[part], sems.at[part]) for part in range(2)]


def spread_rows(moved, wide, slots_by):
    slots = slots_by.shape[0]
    width = moved.shape[1]
    rows = moved.shape[0] // slots
    pitch = slots + 1
    slots_a_step = 32

    def step(index, carry):
        at = index * slots_a_step
        values = moved[pl.ds(pl.multiple_of(at * rows, slots_a_step * rows), slots_a_step * rows), :].astype(F32)
        for slot in range(slots_a_step):
            wide[pl.ds(at + slot, rows, stride=pitch), :] = values[slot * rows : (slot + 1) * rows]
        return carry

    lax.fori_loop(0, slots // slots_a_step, step, 0)
    for row in range(rows):
        slots_by[:, row * width : (row + 1) * width] = wide[row * pitch : row * pitch + slots, :].astype(BF16)


def order_block(start, chooser, slots_by, matrices, mine, width, occupied):
    ordered = jnp.dot(
        chooser[start * occupied : (start + KS_A_BLOCK) * occupied, :], slots_by[...], preferred_element_type=F32
    ).astype(BF16)
    for k in range(KS_A_BLOCK):
        for row in range(slots_by.shape[1] // width):
            at = slice(row * occupied, (row + 1) * occupied)
            lanes = slice((start + k) * width, (start + k + 1) * width)
            block = ordered[k * occupied : (k + 1) * occupied, row * width : (row + 1) * width]
            matrices[at, lanes] = block if mine is None else mine[at, lanes] + block


def choose(chooser, table, occupied):
    pairs, slots = chooser.shape
    lanes = 128
    row = lax.broadcasted_iota(jnp.int32, (pairs, lanes), 0)
    wanted = row % occupied * (pairs // occupied) + row // occupied
    for start in range(0, slots, lanes):
        chooser[:, start : start + lanes] = (table[:, start : start + lanes] == wanted).astype(BF16)


def order_kernel(place, moved, tables, integrals, matrices, slabs, there, here, wide, slots_by, sems, *, occupied):
    copies = slab_copies(place, 0, integrals, slabs, sems)
    for copy in copies:
        copy.start()
    core = (place[0] // 2) % 2
    choose(here, tables[core], occupied)
    spread_rows(moved, wide, slots_by)
    for start in range(0, here.shape[0] // occupied, KS_A_BLOCK):
        order_block(start, here, slots_by, matrices, None, moved.shape[1], occupied)
    choose(there, tables[1 - core], occupied)
    for copy in copies:
        copy.wait()


def order(place, moved, tables, integrals, occupied):
    slots = tables.shape[2]
    pairs = 2 * slots
    width = moved.shape[1]
    rows = moved.shape[0] // slots
    return pl.pallas_call(
        functools.partial(order_kernel, occupied=occupied),
        out_shape=(
            pltpu.VMEM((rows * occupied, pairs // occupied * width), BF16),
            pltpu.VMEM((2,) + integrals.shape[2:], BF16),
            pltpu.VMEM((pairs, slots), BF16),
        ),
        in_specs=[IN_SMEM, IN_VMEM, IN_VMEM, IN_HBM],
        out_specs=(IN_VMEM,) * 3,
        scratch_shapes=[
            pltpu.VMEM((pairs, slots), BF16),
            pltpu.VMEM(((slots + 1) * rows, width), F32),
            pltpu.VMEM((slots, rows * width), BF16),
            pltpu.SemaphoreType.DMA((2,)),
        ],
        compiler_params=PARAMS,
        cost_estimate=cost(2 * pairs * slots * rows * width, integrals.size),
        name="order",
    )(place, moved, tables, integrals)


def product_into(out, matrices, slabs, copies=()):
    half = matrices.shape[0] // 2
    for copy in copies[:1]:
        copy.wait()
    by_real = jnp.dot(matrices[...], slabs[0], preferred_element_type=F32)
    for copy in copies[1:]:
        copy.wait()
    by_imag = jnp.dot(matrices[...], slabs[1], preferred_element_type=F32)
    out[:half] = by_real[:half] - by_imag[half:]
    out[half:] = by_real[half:] + by_imag[:half]


def first_kernel(mine, moved, chooser, slabs, matrices, out, wide, slots_by, by_real, by_imag, *, occupied):
    half = matrices.shape[0] // 2
    width = moved.shape[1]
    spread_rows(moved, wide, slots_by)
    for start in range(0, chooser.shape[0] // occupied, KS_A_BLOCK):
        order_block(start, chooser, slots_by, matrices, mine, width, occupied)
        lanes = slice(start * width, (start + KS_A_BLOCK) * width)
        for part, total in enumerate((by_real, by_imag)):
            product = jnp.dot(matrices[:, lanes], slabs[part, lanes], preferred_element_type=F32)
            total[...] = product if start == 0 else total[...] + product
    out[:half] = by_real[:half] - by_imag[half:]
    out[half:] = by_real[half:] + by_imag[:half]


def first_window(mine, moved, chooser, slabs, occupied):
    width = moved.shape[1]
    slots = chooser.shape[1]
    rows = moved.shape[0] // slots
    full_virtual = slabs.shape[-1]
    return pl.pallas_call(
        functools.partial(first_kernel, occupied=occupied),
        out_shape=(
            jax.ShapeDtypeStruct(mine.shape, BF16),
            jax.ShapeDtypeStruct((mine.shape[0], full_virtual), F32),
        ),
        in_specs=[IN_VMEM] * 4,
        out_specs=(IN_VMEM,) * 2,
        scratch_shapes=[
            pltpu.VMEM(((slots + 1) * rows, width), F32),
            pltpu.VMEM((slots, rows * width), BF16),
            pltpu.VMEM((mine.shape[0], full_virtual), F32),
            pltpu.VMEM((mine.shape[0], full_virtual), F32),
        ],
        compiler_params=PARAMS,
        cost_estimate=cost(4 * mine.size * full_virtual, 4 * mine.size),
        name="first_window",
    )(mine, moved, chooser, pltpu.with_memory_space_constraint(slabs, pltpu.VMEM))


def second_kernel(place, matrices, integrals, out, slabs, sems):
    copies = slab_copies(place, 1, integrals, slabs, sems)
    for copy in copies:
        copy.start()
    product_into(out, matrices, slabs, copies)


def second_window(place, matrices, integrals):
    depth, full_virtual = integrals.shape[2:]
    return pl.pallas_call(
        second_kernel,
        out_shape=jax.ShapeDtypeStruct((matrices.shape[0], full_virtual), F32),
        in_specs=[IN_SMEM, IN_VMEM, IN_HBM],
        out_specs=IN_VMEM,
        scratch_shapes=[pltpu.VMEM((2, depth, full_virtual), BF16), pltpu.SemaphoreType.DMA((2,))],
        compiler_params=PARAMS,
        cost_estimate=cost(4 * matrices.size * full_virtual, 4 * matrices.size),
        name="second_window",
    )(place, matrices, integrals)


def chosen(values, order_by):
    high = values.astype(BF16)
    rest = values - high.astype(F32)
    middle = rest.astype(BF16)
    low = (rest - middle.astype(F32)).astype(BF16)
    total = lax.dot_general(low, order_by, NT, preferred_element_type=F32)
    total += lax.dot_general(middle, order_by, NT, preferred_element_type=F32)
    return total + lax.dot_general(high, order_by, NT, preferred_element_type=F32)


def combine_kernel(kept, got, natural_order, chip_order, own, mirror):
    full_virtual = kept.shape[1]
    rows = kept.shape[0] // 2
    chips = mirror.shape[0] // 8
    here = full_virtual // chips
    occupied = rows // here
    lane = lax.broadcasted_iota(jnp.int32, (occupied, 2 * chips), 1)
    values = kept[...] + got[...]
    by_chip = chosen(values, chip_order[...])
    own[...] = chosen(values, natural_order[...])
    for part in range(2):
        for row in range(0, here, 2):
            at = part * rows + row * occupied
            blocks = []
            for other in range(0, here, 2):
                lanes = slice(other * chips, (other + 2) * chips)
                low = by_chip[at : at + occupied, lanes]
                high = by_chip[at + occupied : at + 2 * occupied, lanes]
                blocks.append(jnp.where(lane < chips, low, pltpu.roll(high, chips, 1)))
                blocks.append(jnp.where(lane < chips, pltpu.roll(low, chips, 1), high))
            turned = jnp.concatenate(blocks, axis=0).T
            mirror[pl.ds(2 * row + part, chips, stride=8), :] = turned[:chips]
            mirror[pl.ds(2 * (row + 1) + part, chips, stride=8), :] = turned[chips:]


def combine(kept, got, natural_order, chip_order, chips):
    return pl.pallas_call(
        combine_kernel,
        out_shape=(jax.ShapeDtypeStruct(kept.shape, F32), jax.ShapeDtypeStruct((chips * 8, kept.shape[0] // 2), F32)),
        compiler_params=PARAMS,
        name="combine",
    )(kept, got, natural_order, chip_order)


def subtract_kernel(place, own, mirror, keep, to_core, to_vir, to_both, block):
    vir, core = place[0] % 2, (place[0] // 2) % 2
    here = 2 * block.shape[1]
    rows, full_virtual = own.shape[0] // 2, own.shape[1]
    occupied = rows // here
    half = full_virtual // 2
    lanes = (slice(0, half), slice(half, full_virtual))
    for part in range(2):
        values = own[part * rows : (part + 1) * rows] - mirror[pl.ds(part, full_virtual, stride=2), :].T
        for row in range(here):
            for side in range(2):
                block[part, row // 2, side, pl.ds(row % 2, occupied, stride=2), :] = values[
                    row * occupied : (row + 1) * occupied, lanes[side]
                ]
    for target, to_side, to_half in (
        (keep, core, vir),
        (to_core, 1 - core, vir),
        (to_vir, core, 1 - vir),
        (to_both, 1 - core, 1 - vir),
    ):
        for part in range(2):
            target[part] = block[part, to_side, to_half].astype(BF16)


def subtract(place, own, mirror):
    rows, full_virtual = own.shape[0] // 2, own.shape[1]
    piece = jax.ShapeDtypeStruct((2, rows // 2, full_virtual // 2), BF16)
    return pl.pallas_call(
        subtract_kernel,
        out_shape=(piece,) * 4,
        in_specs=[IN_SMEM, IN_VMEM, IN_VMEM],
        out_specs=(IN_VMEM,) * 4,
        scratch_shapes=[pltpu.VMEM((2, 2, 2, rows // 2, full_virtual // 2), F32)],
        compiler_params=PARAMS,
        name="subtract",
    )(place, own, mirror)


def finish_kernel(place, keep, from_core, from_vir, from_both, out):
    vir, core = place[0] % 2, (place[0] // 2) % 2
    out[:, 2 * core + vir] = keep[...]
    out[:, 2 * (1 - core) + vir] = from_core[...]
    out[:, 2 * core + 1 - vir] = from_vir[...]
    out[:, 2 * (1 - core) + 1 - vir] = from_both[...]


def finish(place, pieces):
    _, rows, width = pieces[0].shape
    return pl.pallas_call(
        finish_kernel,
        out_shape=jax.ShapeDtypeStruct((2, 4, rows, width), BF16),
        in_specs=[IN_SMEM] + [IN_VMEM] * 4,
        out_specs=IN_VMEM,
        compiler_params=PARAMS,
        name="finish",
    )(place, *pieces)


SWAP = [(0, 1), (1, 0)]
SWAP_BOTH = [(0, 3), (1, 2), (2, 1), (3, 0)]


def body(amplitudes, integrals, pair_table, kramers):
    chips = lax.axis_size("chip")
    place = lax.axis_index(("chip", "core", "vir")).astype(jnp.int32).reshape(1)
    windows, summed_occ = integrals.shape[1:3]
    pairs = pair_table.shape[0]
    occupied = pairs // summed_occ
    slots, full_virtual, width = amplitudes.shape[1:]
    here = full_virtual // chips

    pieces = regroup(amplitudes, chips)
    moved = lax.all_to_all(pieces, "chip", split_axis=0, concat_axis=0, tiled=True)
    moved = moved.reshape(-1, width)
    flat = integrals.reshape(2, windows, summed_occ * integrals.shape[3], full_virtual)
    flat = pltpu.with_memory_space_constraint(flat, pltpu.HBM)
    across = lax.ppermute(moved, "core", SWAP)

    tables = pair_table.reshape(chips, 2, slots).transpose(1, 0, 2).reshape(2, 1, chips * slots)
    places = jnp.arange(full_virtual, dtype=jnp.int32)[:, None]
    natural_order = (kramers[None, :] == places).astype(BF16)
    chip_order = (kramers[None, :] == places % chips * here + places // chips).astype(BF16)

    mine, slabs, chooser = order(place, moved, tables, flat, occupied)
    matrices, to_send = first_window(mine, across, chooser, slabs, occupied)
    got = lax.ppermute(to_send, "vir", SWAP)
    kept = second_window(place, matrices, flat)
    own, mirror = combine(kept, got, natural_order, chip_order, chips)
    mirror = lax.all_to_all(mirror.reshape(chips, 8, -1), "chip", split_axis=0, concat_axis=0, tiled=True)
    keep, to_core, to_vir, to_both = subtract(place, own, mirror.reshape(chips * 8, -1))
    from_vir = lax.ppermute(to_vir, "vir", SWAP)
    from_both = lax.ppermute(to_both, ("core", "vir"), SWAP_BOTH)
    from_core = lax.ppermute(to_core, "core", SWAP)
    got_pieces = (keep, from_core, from_vir, from_both)
    out = finish(place, got_pieces)
    return out.reshape(2, windows, occupied, here // 2, width)


def solution(mesh):
    pair, vir = mesh.devices.shape
    split = Mesh(mesh.devices.reshape(pair // 2, 2, vir), ("chip", "core", "vir"))
    over_pair = ("chip", "core")
    placed = (P(None, over_pair, None, "vir"), P(None, None, None, "vir", None), P(), P())
    return jax.shard_map(
        body,
        mesh=split,
        in_specs=placed,
        out_specs=P(None, None, None, over_pair, "vir"),
        check_vma=False,
    )
```

```python
import functools

import jax
import jax.numpy as jnp
from jax import lax
from jax.experimental import pallas as pl
from jax.experimental.pallas import tpu as pltpu
from jax.sharding import Mesh
from jax.sharding import PartitionSpec as P

F32 = jnp.float32
BF16 = jnp.bfloat16
NT = (((1,), (1,)), ((), ()))
VMEM_LIMIT = 24 * 1024 * 1024
IN_VMEM = pl.BlockSpec(memory_space=pltpu.VMEM)
KS_A_BLOCK = 8
IN_HBM = pl.BlockSpec(memory_space=pl.ANY)
IN_SMEM = pl.BlockSpec(memory_space=pltpu.SMEM)
PARAMS = pltpu.CompilerParams(vmem_limit_bytes=VMEM_LIMIT)


def cost(flops, moved_bytes):
    return pl.CostEstimate(flops=int(flops), bytes_accessed=int(moved_bytes), transcendentals=0)


def regroup_kernel(src, dst, planes, sems):
    parts, slots = src.shape[:2]
    copies = [
        pltpu.make_async_copy(src.at[part, slot], planes.at[part, slot], sems.at[part, slot])
        for part in range(parts)
        for slot in range(slots)
    ]
    for copy in copies:
        copy.start()
    for part in range(parts):
        for slot in range(slots):
            copies[part * slots + slot].wait()
            dst[:, slot * parts + part] = planes[part, slot]


def regroup(amplitudes, chips):
    parts, slots, rows, width = amplitudes.shape
    here = rows // chips
    planes = amplitudes.reshape(parts, slots, chips, here, width)
    return pl.pallas_call(
        regroup_kernel,
        out_shape=jax.ShapeDtypeStruct((chips, parts * slots, here, width), amplitudes.dtype),
        in_specs=[IN_HBM],
        out_specs=IN_VMEM,
        scratch_shapes=[pltpu.VMEM(planes.shape, planes.dtype), pltpu.SemaphoreType.DMA((parts, slots))],
        compiler_params=PARAMS,
        name="regroup",
    )(pltpu.with_memory_space_constraint(planes, pltpu.HBM))


def slab_copies(place, turn, integrals, slabs, sems):
    vir, core = place[0] % 2, (place[0] // 2) % 2
    window = 2 * core + (1 - vir if turn == 0 else vir)
    return [pltpu.make_async_copy(integrals.at[part, window], slabs.at[part], sems.at[part]) for part in range(2)]


def spread_rows(moved, wide, slots_by):
    slots = slots_by.shape[0]
    width = moved.shape[1]
    rows = moved.shape[0] // slots
    pitch = slots + 1
    slots_a_step = 32

    def step(index, carry):
        at = index * slots_a_step
        values = moved[pl.ds(pl.multiple_of(at * rows, slots_a_step * rows), slots_a_step * rows), :].astype(F32)
        for slot in range(slots_a_step):
            wide[pl.ds(at + slot, rows, stride=pitch), :] = values[slot * rows : (slot + 1) * rows]
        return carry

    lax.fori_loop(0, slots // slots_a_step, step, 0)
    for row in range(rows):
        slots_by[:, row * width : (row + 1) * width] = wide[row * pitch : row * pitch + slots, :].astype(BF16)


def order_block(start, chooser, slots_by, matrices, mine, width, occupied):
    ordered = jnp.dot(
        chooser[start * occupied : (start + KS_A_BLOCK) * occupied, :], slots_by[...], preferred_element_type=F32
    ).astype(BF16)
    for k in range(KS_A_BLOCK):
        for row in range(slots_by.shape[1] // width):
            at = slice(row * occupied, (row + 1) * occupied)
            lanes = slice((start + k) * width, (start + k + 1) * width)
            block = ordered[k * occupied : (k + 1) * occupied, row * width : (row + 1) * width]
            matrices[at, lanes] = block if mine is None else mine[at, lanes] + block


def choose(chooser, table, occupied):
    pairs, slots = chooser.shape
    lanes = 128
    row = lax.broadcasted_iota(jnp.int32, (pairs, lanes), 0)
    wanted = row % occupied * (pairs // occupied) + row // occupied
    for start in range(0, slots, lanes):
        chooser[:, start : start + lanes] = (table[:, start : start + lanes] == wanted).astype(BF16)


def order_kernel(place, moved, tables, integrals, matrices, slabs, there, here, wide, slots_by, sems, *, occupied):
    copies = slab_copies(place, 0, integrals, slabs, sems)
    for copy in copies:
        copy.start()
    core = (place[0] // 2) % 2
    choose(here, tables[core], occupied)
    spread_rows(moved, wide, slots_by)
    for start in range(0, here.shape[0] // occupied, KS_A_BLOCK):
        order_block(start, here, slots_by, matrices, None, moved.shape[1], occupied)
    choose(there, tables[1 - core], occupied)
    for copy in copies:
        copy.wait()


def order(place, moved, tables, integrals, occupied):
    slots = tables.shape[2]
    pairs = 2 * slots
    width = moved.shape[1]
    rows = moved.shape[0] // slots
    return pl.pallas_call(
        functools.partial(order_kernel, occupied=occupied),
        out_shape=(
            pltpu.VMEM((rows * occupied, pairs // occupied * width), BF16),
            pltpu.VMEM((2,) + integrals.shape[2:], BF16),
            pltpu.VMEM((pairs, slots), BF16),
        ),
        in_specs=[IN_SMEM, IN_VMEM, IN_VMEM, IN_HBM],
        out_specs=(IN_VMEM,) * 3,
        scratch_shapes=[
            pltpu.VMEM((pairs, slots), BF16),
            pltpu.VMEM(((slots + 1) * rows, width), F32),
            pltpu.VMEM((slots, rows * width), BF16),
            pltpu.SemaphoreType.DMA((2,)),
        ],
        compiler_params=PARAMS,
        cost_estimate=cost(2 * pairs * slots * rows * width, integrals.size),
        name="order",
    )(place, moved, tables, integrals)


def product_into(out, matrices, slabs, copies=()):
    half = matrices.shape[0] // 2
    for copy in copies[:1]:
        copy.wait()
    by_real = jnp.dot(matrices[...], slabs[0], preferred_element_type=F32)
    for copy in copies[1:]:
        copy.wait()
    by_imag = jnp.dot(matrices[...], slabs[1], preferred_element_type=F32)
    out[:half] = by_real[:half] - by_imag[half:]
    out[half:] = by_real[half:] + by_imag[:half]


def first_kernel(mine, moved, chooser, slabs, matrices, out, wide, slots_by, by_real, by_imag, *, occupied):
    half = matrices.shape[0] // 2
    width = moved.shape[1]
    spread_rows(moved, wide, slots_by)
    summed_occ = chooser.shape[0] // occupied
    order_block(0, chooser, slots_by, matrices, mine, width, occupied)
    for start in range(0, summed_occ, KS_A_BLOCK):
        if start + KS_A_BLOCK < summed_occ:
            order_block(start + KS_A_BLOCK, chooser, slots_by, matrices, mine, width, occupied)
        lanes = slice(start * width, (start + KS_A_BLOCK) * width)
        for part, total in enumerate((by_real, by_imag)):
            product = jnp.dot(matrices[:, lanes], slabs[part, lanes], preferred_element_type=F32)
            total[...] = product if start == 0 else total[...] + product
    out[:half] = by_real[:half] - by_imag[half:]
    out[half:] = by_real[half:] + by_imag[:half]


def first_window(mine, moved, chooser, slabs, occupied):
    width = moved.shape[1]
    slots = chooser.shape[1]
    rows = moved.shape[0] // slots
    full_virtual = slabs.shape[-1]
    return pl.pallas_call(
        functools.partial(first_kernel, occupied=occupied),
        out_shape=(
            jax.ShapeDtypeStruct(mine.shape, BF16),
            jax.ShapeDtypeStruct((mine.shape[0], full_virtual), F32),
        ),
        in_specs=[IN_VMEM] * 4,
        out_specs=(IN_VMEM,) * 2,
        scratch_shapes=[
            pltpu.VMEM(((slots + 1) * rows, width), F32),
            pltpu.VMEM((slots, rows * width), BF16),
            pltpu.VMEM((mine.shape[0], full_virtual), F32),
            pltpu.VMEM((mine.shape[0], full_virtual), F32),
        ],
        compiler_params=PARAMS,
        cost_estimate=cost(4 * mine.size * full_virtual, 4 * mine.size),
        name="first_window",
    )(mine, moved, chooser, pltpu.with_memory_space_constraint(slabs, pltpu.VMEM))


def second_kernel(place, matrices, integrals, out, slabs, sems):
    copies = slab_copies(place, 1, integrals, slabs, sems)
    for copy in copies:
        copy.start()
    product_into(out, matrices, slabs, copies)


def second_window(place, matrices, integrals):
    depth, full_virtual = integrals.shape[2:]
    return pl.pallas_call(
        second_kernel,
        out_shape=jax.ShapeDtypeStruct((matrices.shape[0], full_virtual), F32),
        in_specs=[IN_SMEM, IN_VMEM, IN_HBM],
        out_specs=IN_VMEM,
        scratch_shapes=[pltpu.VMEM((2, depth, full_virtual), BF16), pltpu.SemaphoreType.DMA((2,))],
        compiler_params=PARAMS,
        cost_estimate=cost(4 * matrices.size * full_virtual, 4 * matrices.size),
        name="second_window",
    )(place, matrices, integrals)


def chosen(values, order_by):
    high = values.astype(BF16)
    rest = values - high.astype(F32)
    middle = rest.astype(BF16)
    low = (rest - middle.astype(F32)).astype(BF16)
    total = lax.dot_general(low, order_by, NT, preferred_element_type=F32)
    total += lax.dot_general(middle, order_by, NT, preferred_element_type=F32)
    return total + lax.dot_general(high, order_by, NT, preferred_element_type=F32)


def combine_kernel(kept, got, natural_order, chip_order, own, mirror):
    full_virtual = kept.shape[1]
    rows = kept.shape[0] // 2
    chips = mirror.shape[0] // 8
    here = full_virtual // chips
    occupied = rows // here
    lane = lax.broadcasted_iota(jnp.int32, (occupied, 2 * chips), 1)
    values = kept[...] + got[...]
    by_chip = chosen(values, chip_order[...])
    own[...] = chosen(values, natural_order[...])
    for part in range(2):
        for row in range(0, here, 2):
            at = part * rows + row * occupied
            blocks = []
            for other in range(0, here, 2):
                lanes = slice(other * chips, (other + 2) * chips)
                low = by_chip[at : at + occupied, lanes]
                high = by_chip[at + occupied : at + 2 * occupied, lanes]
                blocks.append(jnp.where(lane < chips, low, pltpu.roll(high, chips, 1)))
                blocks.append(jnp.where(lane < chips, pltpu.roll(low, chips, 1), high))
            turned = jnp.concatenate(blocks, axis=0).T
            mirror[pl.ds(2 * row + part, chips, stride=8), :] = turned[:chips]
            mirror[pl.ds(2 * (row + 1) + part, chips, stride=8), :] = turned[chips:]


def combine(kept, got, natural_order, chip_order, chips):
    return pl.pallas_call(
        combine_kernel,
        out_shape=(jax.ShapeDtypeStruct(kept.shape, F32), jax.ShapeDtypeStruct((chips * 8, kept.shape[0] // 2), F32)),
        compiler_params=PARAMS,
        name="combine",
    )(kept, got, natural_order, chip_order)


def subtract_kernel(place, own, mirror, keep, to_core, to_vir, to_both, block):
    vir, core = place[0] % 2, (place[0] // 2) % 2
    here = 2 * block.shape[1]
    rows, full_virtual = own.shape[0] // 2, own.shape[1]
    occupied = rows // here
    half = full_virtual // 2
    lanes = (slice(0, half), slice(half, full_virtual))
    for part in range(2):
        values = own[part * rows : (part + 1) * rows] - mirror[pl.ds(part, full_virtual, stride=2), :].T
        for row in range(here):
            for side in range(2):
                block[part, row // 2, side, pl.ds(row % 2, occupied, stride=2), :] = values[
                    row * occupied : (row + 1) * occupied, lanes[side]
                ]
    for target, to_side, to_half in (
        (keep, core, vir),
        (to_core, 1 - core, vir),
        (to_vir, core, 1 - vir),
        (to_both, 1 - core, 1 - vir),
    ):
        for part in range(2):
            target[part] = block[part, to_side, to_half].astype(BF16)


def subtract(place, own, mirror):
    rows, full_virtual = own.shape[0] // 2, own.shape[1]
    piece = jax.ShapeDtypeStruct((2, rows // 2, full_virtual // 2), BF16)
    return pl.pallas_call(
        subtract_kernel,
        out_shape=(piece,) * 4,
        in_specs=[IN_SMEM, IN_VMEM, IN_VMEM],
        out_specs=(IN_VMEM,) * 4,
        scratch_shapes=[pltpu.VMEM((2, 2, 2, rows // 2, full_virtual // 2), F32)],
        compiler_params=PARAMS,
        name="subtract",
    )(place, own, mirror)


def finish_kernel(place, keep, from_core, from_vir, from_both, out):
    vir, core = place[0] % 2, (place[0] // 2) % 2
    out[:, 2 * core + vir] = keep[...]
    out[:, 2 * (1 - core) + vir] = from_core[...]
    out[:, 2 * core + 1 - vir] = from_vir[...]
    out[:, 2 * (1 - core) + 1 - vir] = from_both[...]


def finish(place, pieces):
    _, rows, width = pieces[0].shape
    return pl.pallas_call(
        finish_kernel,
        out_shape=jax.ShapeDtypeStruct((2, 4, rows, width), BF16),
        in_specs=[IN_SMEM] + [IN_VMEM] * 4,
        out_specs=IN_VMEM,
        compiler_params=PARAMS,
        name="finish",
    )(place, *pieces)


SWAP = [(0, 1), (1, 0)]
SWAP_BOTH = [(0, 3), (1, 2), (2, 1), (3, 0)]


def body(amplitudes, integrals, pair_table, kramers):
    chips = lax.axis_size("chip")
    place = lax.axis_index(("chip", "core", "vir")).astype(jnp.int32).reshape(1)
    windows, summed_occ = integrals.shape[1:3]
    pairs = pair_table.shape[0]
    occupied = pairs // summed_occ
    slots, full_virtual, width = amplitudes.shape[1:]
    here = full_virtual // chips

    pieces = regroup(amplitudes, chips)
    moved = lax.all_to_all(pieces, "chip", split_axis=0, concat_axis=0, tiled=True)
    moved = moved.reshape(-1, width)
    flat = integrals.reshape(2, windows, summed_occ * integrals.shape[3], full_virtual)
    flat = pltpu.with_memory_space_constraint(flat, pltpu.HBM)
    across = lax.ppermute(moved, "core", SWAP)

    tables = pair_table.reshape(chips, 2, slots).transpose(1, 0, 2).reshape(2, 1, chips * slots)
    places = jnp.arange(full_virtual, dtype=jnp.int32)[:, None]
    natural_order = (kramers[None, :] == places).astype(BF16)
    chip_order = (kramers[None, :] == places % chips * here + places // chips).astype(BF16)

    mine, slabs, chooser = order(place, moved, tables, flat, occupied)
    matrices, to_send = first_window(mine, across, chooser, slabs, occupied)
    got = lax.ppermute(to_send, "vir", SWAP)
    kept = second_window(place, matrices, flat)
    own, mirror = combine(kept, got, natural_order, chip_order, chips)
    mirror = lax.all_to_all(mirror.reshape(chips, 8, -1), "chip", split_axis=0, concat_axis=0, tiled=True)
    keep, to_core, to_vir, to_both = subtract(place, own, mirror.reshape(chips * 8, -1))
    from_vir = lax.ppermute(to_vir, "vir", SWAP)
    from_both = lax.ppermute(to_both, ("core", "vir"), SWAP_BOTH)
    from_core = lax.ppermute(to_core, "core", SWAP)
    got_pieces = (keep, from_core, from_vir, from_both)
    out = finish(place, got_pieces)
    return out.reshape(2, windows, occupied, here // 2, width)


def solution(mesh):
    pair, vir = mesh.devices.shape
    split = Mesh(mesh.devices.reshape(pair // 2, 2, vir), ("chip", "core", "vir"))
    over_pair = ("chip", "core")
    placed = (P(None, over_pair, None, "vir"), P(None, None, None, "vir", None), P(), P())
    return jax.shard_map(
        body,
        mesh=split,
        in_specs=placed,
        out_specs=P(None, None, None, over_pair, "vir"),
        check_vma=False,
    )
```

```python
import functools

import jax
import jax.numpy as jnp
from jax import lax
from jax.experimental import pallas as pl
from jax.experimental.pallas import tpu as pltpu
from jax.sharding import Mesh
from jax.sharding import PartitionSpec as P

F32 = jnp.float32
BF16 = jnp.bfloat16
NT = (((1,), (1,)), ((), ()))
VMEM_LIMIT = 24 * 1024 * 1024
IN_VMEM = pl.BlockSpec(memory_space=pltpu.VMEM)
KS_A_BLOCK = 8
IN_HBM = pl.BlockSpec(memory_space=pl.ANY)
IN_SMEM = pl.BlockSpec(memory_space=pltpu.SMEM)
PARAMS = pltpu.CompilerParams(vmem_limit_bytes=VMEM_LIMIT)


def cost(flops, moved_bytes):
    return pl.CostEstimate(flops=int(flops), bytes_accessed=int(moved_bytes), transcendentals=0)


def regroup_kernel(src, dst, planes, sems):
    parts, slots = src.shape[:2]
    copies = [
        pltpu.make_async_copy(src.at[part, slot], planes.at[part, slot], sems.at[part, slot])
        for part in range(parts)
        for slot in range(slots)
    ]
    for copy in copies:
        copy.start()
    for part in range(parts):
        for slot in range(slots):
            copies[part * slots + slot].wait()
            dst[:, slot * parts + part] = planes[part, slot]


def regroup(amplitudes, chips):
    parts, slots, rows, width = amplitudes.shape
    here = rows // chips
    planes = amplitudes.reshape(parts, slots, chips, here, width)
    return pl.pallas_call(
        regroup_kernel,
        out_shape=jax.ShapeDtypeStruct((chips, parts * slots, here, width), amplitudes.dtype),
        in_specs=[IN_HBM],
        out_specs=IN_VMEM,
        scratch_shapes=[pltpu.VMEM(planes.shape, planes.dtype), pltpu.SemaphoreType.DMA((parts, slots))],
        compiler_params=PARAMS,
        name="regroup",
    )(pltpu.with_memory_space_constraint(planes, pltpu.HBM))


def slab_copies(place, turn, integrals, slabs, sems):
    vir, core = place[0] % 2, (place[0] // 2) % 2
    window = 2 * core + (1 - vir if turn == 0 else vir)
    return [pltpu.make_async_copy(integrals.at[part, window], slabs.at[part], sems.at[part]) for part in range(2)]


def spread_rows(moved, wide, slots_by):
    slots = slots_by.shape[0]
    width = moved.shape[1]
    rows = moved.shape[0] // slots
    pitch = slots + 1
    slots_a_step = 32

    def step(index, carry):
        at = index * slots_a_step
        values = moved[pl.ds(pl.multiple_of(at * rows, slots_a_step * rows), slots_a_step * rows), :].astype(F32)
        for slot in range(slots_a_step):
            wide[pl.ds(at + slot, rows, stride=pitch), :] = values[slot * rows : (slot + 1) * rows]
        return carry

    lax.fori_loop(0, slots // slots_a_step, step, 0)
    for row in range(rows):
        slots_by[:, row * width : (row + 1) * width] = wide[row * pitch : row * pitch + slots, :].astype(BF16)


def order_block(start, chooser, slots_by, matrices, mine, width, occupied):
    ordered = jnp.dot(
        chooser[start * occupied : (start + KS_A_BLOCK) * occupied, :], slots_by[...], preferred_element_type=F32
    ).astype(BF16)
    for k in range(KS_A_BLOCK):
        for row in range(slots_by.shape[1] // width):
            at = slice(row * occupied, (row + 1) * occupied)
            lanes = slice((start + k) * width, (start + k + 1) * width)
            block = ordered[k * occupied : (k + 1) * occupied, row * width : (row + 1) * width]
            matrices[at, lanes] = block if mine is None else mine[at, lanes] + block


def choose(chooser, table, occupied):
    pairs, slots = chooser.shape
    lanes = 128
    row = lax.broadcasted_iota(jnp.int32, (pairs, lanes), 0)
    wanted = row % occupied * (pairs // occupied) + row // occupied
    for start in range(0, slots, lanes):
        chooser[:, start : start + lanes] = (table[:, start : start + lanes] == wanted).astype(BF16)


def order_kernel(place, moved, tables, integrals, matrices, slabs, there, here, wide, slots_by, sems, *, occupied):
    copies = slab_copies(place, 0, integrals, slabs, sems)
    for copy in copies:
        copy.start()
    core = (place[0] // 2) % 2
    choose(here, tables[core], occupied)
    spread_rows(moved, wide, slots_by)
    for start in range(0, here.shape[0] // occupied, KS_A_BLOCK):
        order_block(start, here, slots_by, matrices, None, moved.shape[1], occupied)
    choose(there, tables[1 - core], occupied)
    for copy in copies:
        copy.wait()


def order(place, moved, tables, integrals, occupied):
    slots = tables.shape[2]
    pairs = 2 * slots
    width = moved.shape[1]
    rows = moved.shape[0] // slots
    return pl.pallas_call(
        functools.partial(order_kernel, occupied=occupied),
        out_shape=(
            pltpu.VMEM((rows * occupied, pairs // occupied * width), BF16),
            pltpu.VMEM((2,) + integrals.shape[2:], BF16),
            pltpu.VMEM((pairs, slots), BF16),
        ),
        in_specs=[IN_SMEM, IN_VMEM, IN_VMEM, IN_HBM],
        out_specs=(IN_VMEM,) * 3,
        scratch_shapes=[
            pltpu.VMEM((pairs, slots), BF16),
            pltpu.VMEM(((slots + 1) * rows, width), F32),
            pltpu.VMEM((slots, rows * width), BF16),
            pltpu.SemaphoreType.DMA((2,)),
        ],
        compiler_params=PARAMS,
        cost_estimate=cost(2 * pairs * slots * rows * width, integrals.size),
        name="order",
    )(place, moved, tables, integrals)


def product_into(out, matrices, slabs, copies=()):
    half = matrices.shape[0] // 2
    for copy in copies[:1]:
        copy.wait()
    by_real = jnp.dot(matrices[...], slabs[0], preferred_element_type=F32)
    for copy in copies[1:]:
        copy.wait()
    by_imag = jnp.dot(matrices[...], slabs[1], preferred_element_type=F32)
    out[:half] = by_real[:half] - by_imag[half:]
    out[half:] = by_real[half:] + by_imag[:half]


def first_kernel(
    place, mine, moved, chooser, slabs, integrals, matrices, out, early, wide, slots_by, by_real, by_imag, own_slabs, sems, *, occupied
):
    copies = slab_copies(place, 1, integrals, own_slabs, sems)
    core = (place[0] // 2) % 2

    @pl.when(core == 1)
    def _():
        for copy in copies:
            copy.start()

    half = matrices.shape[0] // 2
    width = moved.shape[1]
    spread_rows(moved, wide, slots_by)
    summed_occ = chooser.shape[0] // occupied
    order_block(0, chooser, slots_by, matrices, mine, width, occupied)
    for start in range(0, summed_occ, KS_A_BLOCK):
        if start + KS_A_BLOCK < summed_occ:
            order_block(start + KS_A_BLOCK, chooser, slots_by, matrices, mine, width, occupied)
        lanes = slice(start * width, (start + KS_A_BLOCK) * width)
        for part, total in enumerate((by_real, by_imag)):
            product = jnp.dot(matrices[:, lanes], slabs[part, lanes], preferred_element_type=F32)
            total[...] = product if start == 0 else total[...] + product
    out[:half] = by_real[:half] - by_imag[half:]
    out[half:] = by_real[half:] + by_imag[:half]

    @pl.when(core == 1)
    def _():
        product_into(early, matrices, own_slabs, copies)


def first_window(place, mine, moved, chooser, slabs, integrals, occupied):
    width = moved.shape[1]
    slots = chooser.shape[1]
    rows = moved.shape[0] // slots
    full_virtual = slabs.shape[-1]
    return pl.pallas_call(
        functools.partial(first_kernel, occupied=occupied),
        out_shape=(
            jax.ShapeDtypeStruct(mine.shape, BF16),
            jax.ShapeDtypeStruct((mine.shape[0], full_virtual), F32),
            jax.ShapeDtypeStruct((mine.shape[0], full_virtual), F32),
        ),
        in_specs=[IN_SMEM] + [IN_VMEM] * 4 + [IN_HBM],
        out_specs=(IN_VMEM,) * 3,
        scratch_shapes=[
            pltpu.VMEM(((slots + 1) * rows, width), F32),
            pltpu.VMEM((slots, rows * width), BF16),
            pltpu.VMEM((mine.shape[0], full_virtual), F32),
            pltpu.VMEM((mine.shape[0], full_virtual), F32),
            pltpu.VMEM(slabs.shape, BF16),
            pltpu.SemaphoreType.DMA((2,)),
        ],
        compiler_params=PARAMS,
        cost_estimate=cost(4 * mine.size * full_virtual, 4 * mine.size),
        name="first_window",
    )(place, mine, moved, chooser, pltpu.with_memory_space_constraint(slabs, pltpu.VMEM), integrals)


def second_kernel(place, matrices, early, integrals, out, slabs, sems):
    copies = slab_copies(place, 1, integrals, slabs, sems)
    core = (place[0] // 2) % 2

    @pl.when(core == 0)
    def _():
        for copy in copies:
            copy.start()
        product_into(out, matrices, slabs, copies)

    @pl.when(core == 1)
    def _():
        out[...] = early[...]


def second_window(place, matrices, early, integrals):
    depth, full_virtual = integrals.shape[2:]
    return pl.pallas_call(
        second_kernel,
        out_shape=jax.ShapeDtypeStruct((matrices.shape[0], full_virtual), F32),
        in_specs=[IN_SMEM, IN_VMEM, IN_VMEM, IN_HBM],
        out_specs=IN_VMEM,
        scratch_shapes=[pltpu.VMEM((2, depth, full_virtual), BF16), pltpu.SemaphoreType.DMA((2,))],
        compiler_params=PARAMS,
        cost_estimate=cost(4 * matrices.size * full_virtual, 4 * matrices.size),
        name="second_window",
    )(place, matrices, early, integrals)


def chosen(values, order_by):
    high = values.astype(BF16)
    rest = values - high.astype(F32)
    middle = rest.astype(BF16)
    low = (rest - middle.astype(F32)).astype(BF16)
    total = lax.dot_general(low, order_by, NT, preferred_element_type=F32)
    total += lax.dot_general(middle, order_by, NT, preferred_element_type=F32)
    return total + lax.dot_general(high, order_by, NT, preferred_element_type=F32)


def combine_kernel(kept, got, natural_order, chip_order, own, mirror):
    full_virtual = kept.shape[1]
    rows = kept.shape[0] // 2
    chips = mirror.shape[0] // 8
    here = full_virtual // chips
    occupied = rows // here
    lane = lax.broadcasted_iota(jnp.int32, (occupied, 2 * chips), 1)
    values = kept[...] + got[...]
    by_chip = chosen(values, chip_order[...])
    own[...] = chosen(values, natural_order[...])
    for part in range(2):
        for row in range(0, here, 2):
            at = part * rows + row * occupied
            blocks = []
            for other in range(0, here, 2):
                lanes = slice(other * chips, (other + 2) * chips)
                low = by_chip[at : at + occupied, lanes]
                high = by_chip[at + occupied : at + 2 * occupied, lanes]
                blocks.append(jnp.where(lane < chips, low, pltpu.roll(high, chips, 1)))
                blocks.append(jnp.where(lane < chips, pltpu.roll(low, chips, 1), high))
            turned = jnp.concatenate(blocks, axis=0).T
            mirror[pl.ds(2 * row + part, chips, stride=8), :] = turned[:chips]
            mirror[pl.ds(2 * (row + 1) + part, chips, stride=8), :] = turned[chips:]


def combine(kept, got, natural_order, chip_order, chips):
    return pl.pallas_call(
        combine_kernel,
        out_shape=(jax.ShapeDtypeStruct(kept.shape, F32), jax.ShapeDtypeStruct((chips * 8, kept.shape[0] // 2), F32)),
        compiler_params=PARAMS,
        name="combine",
    )(kept, got, natural_order, chip_order)


def subtract_kernel(place, own, mirror, keep, to_core, to_vir, to_both, block):
    vir, core = place[0] % 2, (place[0] // 2) % 2
    here = 2 * block.shape[1]
    rows, full_virtual = own.shape[0] // 2, own.shape[1]
    occupied = rows // here
    half = full_virtual // 2
    lanes = (slice(0, half), slice(half, full_virtual))
    for part in range(2):
        values = own[part * rows : (part + 1) * rows] - mirror[pl.ds(part, full_virtual, stride=2), :].T
        for row in range(here):
            for side in range(2):
                block[part, row // 2, side, pl.ds(row % 2, occupied, stride=2), :] = values[
                    row * occupied : (row + 1) * occupied, lanes[side]
                ]
    for target, to_side, to_half in (
        (keep, core, vir),
        (to_core, 1 - core, vir),
        (to_vir, core, 1 - vir),
        (to_both, 1 - core, 1 - vir),
    ):
        for part in range(2):
            target[part] = block[part, to_side, to_half].astype(BF16)


def subtract(place, own, mirror):
    rows, full_virtual = own.shape[0] // 2, own.shape[1]
    piece = jax.ShapeDtypeStruct((2, rows // 2, full_virtual // 2), BF16)
    return pl.pallas_call(
        subtract_kernel,
        out_shape=(piece,) * 4,
        in_specs=[IN_SMEM, IN_VMEM, IN_VMEM],
        out_specs=(IN_VMEM,) * 4,
        scratch_shapes=[pltpu.VMEM((2, 2, 2, rows // 2, full_virtual // 2), F32)],
        compiler_params=PARAMS,
        name="subtract",
    )(place, own, mirror)


def finish_kernel(place, keep, from_core, from_vir, from_both, out):
    vir, core = place[0] % 2, (place[0] // 2) % 2
    out[:, 2 * core + vir] = keep[...]
    out[:, 2 * (1 - core) + vir] = from_core[...]
    out[:, 2 * core + 1 - vir] = from_vir[...]
    out[:, 2 * (1 - core) + 1 - vir] = from_both[...]


def finish(place, pieces):
    _, rows, width = pieces[0].shape
    return pl.pallas_call(
        finish_kernel,
        out_shape=jax.ShapeDtypeStruct((2, 4, rows, width), BF16),
        in_specs=[IN_SMEM] + [IN_VMEM] * 4,
        out_specs=IN_VMEM,
        compiler_params=PARAMS,
        name="finish",
    )(place, *pieces)


SWAP = [(0, 1), (1, 0)]
SWAP_BOTH = [(0, 3), (1, 2), (2, 1), (3, 0)]


def body(amplitudes, integrals, pair_table, kramers):
    chips = lax.axis_size("chip")
    place = lax.axis_index(("chip", "core", "vir")).astype(jnp.int32).reshape(1)
    windows, summed_occ = integrals.shape[1:3]
    pairs = pair_table.shape[0]
    occupied = pairs // summed_occ
    slots, full_virtual, width = amplitudes.shape[1:]
    here = full_virtual // chips

    pieces = regroup(amplitudes, chips)
    moved = lax.all_to_all(pieces, "chip", split_axis=0, concat_axis=0, tiled=True)
    moved = moved.reshape(-1, width)
    flat = integrals.reshape(2, windows, summed_occ * integrals.shape[3], full_virtual)
    flat = pltpu.with_memory_space_constraint(flat, pltpu.HBM)
    across = lax.ppermute(moved, "core", SWAP)

    tables = pair_table.reshape(chips, 2, slots).transpose(1, 0, 2).reshape(2, 1, chips * slots)
    places = jnp.arange(full_virtual, dtype=jnp.int32)[:, None]
    natural_order = (kramers[None, :] == places).astype(BF16)
    chip_order = (kramers[None, :] == places % chips * here + places // chips).astype(BF16)

    mine, slabs, chooser = order(place, moved, tables, flat, occupied)
    matrices, to_send, early = first_window(place, mine, across, chooser, slabs, flat, occupied)
    got = lax.ppermute(to_send, "vir", SWAP)
    kept = second_window(place, matrices, early, flat)
    own, mirror = combine(kept, got, natural_order, chip_order, chips)
    mirror = lax.all_to_all(mirror.reshape(chips, 8, -1), "chip", split_axis=0, concat_axis=0, tiled=True)
    keep, to_core, to_vir, to_both = subtract(place, own, mirror.reshape(chips * 8, -1))
    from_vir = lax.ppermute(to_vir, "vir", SWAP)
    from_both = lax.ppermute(to_both, ("core", "vir"), SWAP_BOTH)
    from_core = lax.ppermute(to_core, "core", SWAP)
    got_pieces = (keep, from_core, from_vir, from_both)
    out = finish(place, got_pieces)
    return out.reshape(2, windows, occupied, here // 2, width)


def solution(mesh):
    pair, vir = mesh.devices.shape
    split = Mesh(mesh.devices.reshape(pair // 2, 2, vir), ("chip", "core", "vir"))
    over_pair = ("chip", "core")
    placed = (P(None, over_pair, None, "vir"), P(None, None, None, "vir", None), P(), P())
    return jax.shard_map(
        body,
        mesh=split,
        in_specs=placed,
        out_specs=P(None, None, None, over_pair, "vir"),
        check_vma=False,
    )
```

```python
import functools

import jax
import jax.numpy as jnp
from jax import lax
from jax.experimental import pallas as pl
from jax.experimental.pallas import tpu as pltpu
from jax.sharding import Mesh
from jax.sharding import PartitionSpec as P

F32 = jnp.float32
BF16 = jnp.bfloat16
NT = (((1,), (1,)), ((), ()))
VMEM_LIMIT = 24 * 1024 * 1024
IN_VMEM = pl.BlockSpec(memory_space=pltpu.VMEM)
KS_A_BLOCK = 6
IN_HBM = pl.BlockSpec(memory_space=pl.ANY)
IN_SMEM = pl.BlockSpec(memory_space=pltpu.SMEM)
PARAMS = pltpu.CompilerParams(vmem_limit_bytes=VMEM_LIMIT)


def cost(flops, moved_bytes):
    return pl.CostEstimate(flops=int(flops), bytes_accessed=int(moved_bytes), transcendentals=0)


def regroup_kernel(src, dst, planes, sems):
    parts, slots = src.shape[:2]
    copies = [
        pltpu.make_async_copy(src.at[part, slot], planes.at[part, slot], sems.at[part, slot])
        for part in range(parts)
        for slot in range(slots)
    ]
    for copy in copies:
        copy.start()
    for part in range(parts):
        for slot in range(slots):
            copies[part * slots + slot].wait()
            dst[:, slot * parts + part] = planes[part, slot]


def regroup(amplitudes, chips):
    parts, slots, rows, width = amplitudes.shape
    here = rows // chips
    planes = amplitudes.reshape(parts, slots, chips, here, width)
    return pl.pallas_call(
        regroup_kernel,
        out_shape=jax.ShapeDtypeStruct((chips, parts * slots, here, width), amplitudes.dtype),
        in_specs=[IN_HBM],
        out_specs=IN_VMEM,
        scratch_shapes=[pltpu.VMEM(planes.shape, planes.dtype), pltpu.SemaphoreType.DMA((parts, slots))],
        compiler_params=PARAMS,
        name="regroup",
    )(pltpu.with_memory_space_constraint(planes, pltpu.HBM))


def slab_copies(place, turn, integrals, slabs, sems):
    vir, core = place[0] % 2, (place[0] // 2) % 2
    window = 2 * core + (1 - vir if turn == 0 else vir)
    return [pltpu.make_async_copy(integrals.at[part, window], slabs.at[part], sems.at[part]) for part in range(2)]


def spread_rows(moved, wide, slots_by):
    slots = slots_by.shape[0]
    width = moved.shape[1]
    rows = moved.shape[0] // slots
    pitch = slots + 1
    slots_a_step = 32

    def step(index, carry):
        at = index * slots_a_step
        values = moved[pl.ds(pl.multiple_of(at * rows, slots_a_step * rows), slots_a_step * rows), :].astype(F32)
        for slot in range(slots_a_step):
            wide[pl.ds(at + slot, rows, stride=pitch), :] = values[slot * rows : (slot + 1) * rows]
        return carry

    lax.fori_loop(0, slots // slots_a_step, step, 0)
    for row in range(rows):
        slots_by[:, row * width : (row + 1) * width] = wide[row * pitch : row * pitch + slots, :].astype(BF16)


def order_block(start, chooser, slots_by, matrices, mine, width, occupied):
    ordered = jnp.dot(
        chooser[start * occupied : (start + KS_A_BLOCK) * occupied, :], slots_by[...], preferred_element_type=F32
    ).astype(BF16)
    for k in range(KS_A_BLOCK):
        for row in range(slots_by.shape[1] // width):
            at = slice(row * occupied, (row + 1) * occupied)
            lanes = slice((start + k) * width, (start + k + 1) * width)
            block = ordered[k * occupied : (k + 1) * occupied, row * width : (row + 1) * width]
            matrices[at, lanes] = block if mine is None else mine[at, lanes] + block


def choose(chooser, table, occupied):
    pairs, slots = chooser.shape
    lanes = 128
    row = lax.broadcasted_iota(jnp.int32, (pairs, lanes), 0)
    wanted = row % occupied * (pairs // occupied) + row // occupied
    for start in range(0, slots, lanes):
        chooser[:, start : start + lanes] = (table[:, start : start + lanes] == wanted).astype(BF16)


def order_kernel(place, moved, tables, integrals, matrices, slabs, there, here, wide, slots_by, sems, *, occupied):
    copies = slab_copies(place, 0, integrals, slabs, sems)
    for copy in copies:
        copy.start()
    core = (place[0] // 2) % 2
    choose(here, tables[core], occupied)
    spread_rows(moved, wide, slots_by)
    for start in range(0, here.shape[0] // occupied, KS_A_BLOCK):
        order_block(start, here, slots_by, matrices, None, moved.shape[1], occupied)
    choose(there, tables[1 - core], occupied)
    for copy in copies:
        copy.wait()


def order(place, moved, tables, integrals, occupied):
    slots = tables.shape[2]
    pairs = 2 * slots
    width = moved.shape[1]
    rows = moved.shape[0] // slots
    return pl.pallas_call(
        functools.partial(order_kernel, occupied=occupied),
        out_shape=(
            pltpu.VMEM((rows * occupied, pairs // occupied * width), BF16),
            pltpu.VMEM((2,) + integrals.shape[2:], BF16),
            pltpu.VMEM((pairs, slots), BF16),
        ),
        in_specs=[IN_SMEM, IN_VMEM, IN_VMEM, IN_HBM],
        out_specs=(IN_VMEM,) * 3,
        scratch_shapes=[
            pltpu.VMEM((pairs, slots), BF16),
            pltpu.VMEM(((slots + 1) * rows, width), F32),
            pltpu.VMEM((slots, rows * width), BF16),
            pltpu.SemaphoreType.DMA((2,)),
        ],
        compiler_params=PARAMS,
        cost_estimate=cost(2 * pairs * slots * rows * width, integrals.size),
        name="order",
    )(place, moved, tables, integrals)


def product_into(out, matrices, slabs, copies=()):
    half = matrices.shape[0] // 2
    for copy in copies[:1]:
        copy.wait()
    by_real = jnp.dot(matrices[...], slabs[0], preferred_element_type=F32)
    for copy in copies[1:]:
        copy.wait()
    by_imag = jnp.dot(matrices[...], slabs[1], preferred_element_type=F32)
    out[:half] = by_real[:half] - by_imag[half:]
    out[half:] = by_real[half:] + by_imag[:half]


def first_kernel(mine, moved, chooser, slabs, matrices, out, wide, slots_by, by_real, by_imag, *, occupied):
    half = matrices.shape[0] // 2
    width = moved.shape[1]
    spread_rows(moved, wide, slots_by)
    summed_occ = chooser.shape[0] // occupied
    order_block(0, chooser, slots_by, matrices, mine, width, occupied)
    for start in range(0, summed_occ, KS_A_BLOCK):
        if start + KS_A_BLOCK < summed_occ:
            order_block(start + KS_A_BLOCK, chooser, slots_by, matrices, mine, width, occupied)
        lanes = slice(start * width, (start + KS_A_BLOCK) * width)
        for part, total in enumerate((by_real, by_imag)):
            product = jnp.dot(matrices[:, lanes], slabs[part, lanes], preferred_element_type=F32)
            total[...] = product if start == 0 else total[...] + product
    out[:half] = by_real[:half] - by_imag[half:]
    out[half:] = by_real[half:] + by_imag[:half]


def first_window(mine, moved, chooser, slabs, occupied):
    width = moved.shape[1]
    slots = chooser.shape[1]
    rows = moved.shape[0] // slots
    full_virtual = slabs.shape[-1]
    return pl.pallas_call(
        functools.partial(first_kernel, occupied=occupied),
        out_shape=(
            jax.ShapeDtypeStruct(mine.shape, BF16),
            jax.ShapeDtypeStruct((mine.shape[0], full_virtual), F32),
        ),
        in_specs=[IN_VMEM] * 4,
        out_specs=(IN_VMEM,) * 2,
        scratch_shapes=[
            pltpu.VMEM(((slots + 1) * rows, width), F32),
            pltpu.VMEM((slots, rows * width), BF16),
            pltpu.VMEM((mine.shape[0], full_virtual), F32),
            pltpu.VMEM((mine.shape[0], full_virtual), F32),
        ],
        compiler_params=PARAMS,
        cost_estimate=cost(4 * mine.size * full_virtual, 4 * mine.size),
        name="first_window",
    )(mine, moved, chooser, pltpu.with_memory_space_constraint(slabs, pltpu.VMEM))


def second_kernel(place, matrices, integrals, out, slabs, sems):
    copies = slab_copies(place, 1, integrals, slabs, sems)
    for copy in copies:
        copy.start()
    product_into(out, matrices, slabs, copies)


def second_window(place, matrices, integrals):
    depth, full_virtual = integrals.shape[2:]
    return pl.pallas_call(
        second_kernel,
        out_shape=jax.ShapeDtypeStruct((matrices.shape[0], full_virtual), F32),
        in_specs=[IN_SMEM, IN_VMEM, IN_HBM],
        out_specs=IN_VMEM,
        scratch_shapes=[pltpu.VMEM((2, depth, full_virtual), BF16), pltpu.SemaphoreType.DMA((2,))],
        compiler_params=PARAMS,
        cost_estimate=cost(4 * matrices.size * full_virtual, 4 * matrices.size),
        name="second_window",
    )(place, matrices, integrals)


def chosen(values, order_by):
    high = values.astype(BF16)
    rest = values - high.astype(F32)
    middle = rest.astype(BF16)
    low = (rest - middle.astype(F32)).astype(BF16)
    total = lax.dot_general(low, order_by, NT, preferred_element_type=F32)
    total += lax.dot_general(middle, order_by, NT, preferred_element_type=F32)
    return total + lax.dot_general(high, order_by, NT, preferred_element_type=F32)


def combine_kernel(kept, got, natural_order, chip_order, own, mirror):
    full_virtual = kept.shape[1]
    rows = kept.shape[0] // 2
    chips = mirror.shape[0] // 8
    here = full_virtual // chips
    occupied = rows // here
    lane = lax.broadcasted_iota(jnp.int32, (occupied, 2 * chips), 1)
    values = kept[...] + got[...]
    by_chip = chosen(values, chip_order[...])
    own[...] = chosen(values, natural_order[...])
    for part in range(2):
        for row in range(0, here, 2):
            at = part * rows + row * occupied
            blocks = []
            for other in range(0, here, 2):
                lanes = slice(other * chips, (other + 2) * chips)
                low = by_chip[at : at + occupied, lanes]
                high = by_chip[at + occupied : at + 2 * occupied, lanes]
                blocks.append(jnp.where(lane < chips, low, pltpu.roll(high, chips, 1)))
                blocks.append(jnp.where(lane < chips, pltpu.roll(low, chips, 1), high))
            turned = jnp.concatenate(blocks, axis=0).T
            mirror[pl.ds(2 * row + part, chips, stride=8), :] = turned[:chips]
            mirror[pl.ds(2 * (row + 1) + part, chips, stride=8), :] = turned[chips:]


def combine(kept, got, natural_order, chip_order, chips):
    return pl.pallas_call(
        combine_kernel,
        out_shape=(jax.ShapeDtypeStruct(kept.shape, F32), jax.ShapeDtypeStruct((chips * 8, kept.shape[0] // 2), F32)),
        compiler_params=PARAMS,
        name="combine",
    )(kept, got, natural_order, chip_order)


def subtract_kernel(place, own, mirror, keep, to_core, to_vir, to_both, block):
    vir, core = place[0] % 2, (place[0] // 2) % 2
    here = 2 * block.shape[1]
    rows, full_virtual = own.shape[0] // 2, own.shape[1]
    occupied = rows // here
    half = full_virtual // 2
    lanes = (slice(0, half), slice(half, full_virtual))
    for part in range(2):
        values = own[part * rows : (part + 1) * rows] - mirror[pl.ds(part, full_virtual, stride=2), :].T
        for row in range(here):
            for side in range(2):
                block[part, row // 2, side, pl.ds(row % 2, occupied, stride=2), :] = values[
                    row * occupied : (row + 1) * occupied, lanes[side]
                ]
    for target, to_side, to_half in (
        (keep, core, vir),
        (to_core, 1 - core, vir),
        (to_vir, core, 1 - vir),
        (to_both, 1 - core, 1 - vir),
    ):
        for part in range(2):
            target[part] = block[part, to_side, to_half].astype(BF16)


def subtract(place, own, mirror):
    rows, full_virtual = own.shape[0] // 2, own.shape[1]
    piece = jax.ShapeDtypeStruct((2, rows // 2, full_virtual // 2), BF16)
    return pl.pallas_call(
        subtract_kernel,
        out_shape=(piece,) * 4,
        in_specs=[IN_SMEM, IN_VMEM, IN_VMEM],
        out_specs=(IN_VMEM,) * 4,
        scratch_shapes=[pltpu.VMEM((2, 2, 2, rows // 2, full_virtual // 2), F32)],
        compiler_params=PARAMS,
        name="subtract",
    )(place, own, mirror)


def finish_kernel(place, keep, from_core, from_vir, from_both, out):
    vir, core = place[0] % 2, (place[0] // 2) % 2
    out[:, 2 * core + vir] = keep[...]
    out[:, 2 * (1 - core) + vir] = from_core[...]
    out[:, 2 * core + 1 - vir] = from_vir[...]
    out[:, 2 * (1 - core) + 1 - vir] = from_both[...]


def finish(place, pieces):
    _, rows, width = pieces[0].shape
    return pl.pallas_call(
        finish_kernel,
        out_shape=jax.ShapeDtypeStruct((2, 4, rows, width), BF16),
        in_specs=[IN_SMEM] + [IN_VMEM] * 4,
        out_specs=IN_VMEM,
        compiler_params=PARAMS,
        name="finish",
    )(place, *pieces)


SWAP = [(0, 1), (1, 0)]
SWAP_BOTH = [(0, 3), (1, 2), (2, 1), (3, 0)]


def body(amplitudes, integrals, pair_table, kramers):
    chips = lax.axis_size("chip")
    place = lax.axis_index(("chip", "core", "vir")).astype(jnp.int32).reshape(1)
    windows, summed_occ = integrals.shape[1:3]
    pairs = pair_table.shape[0]
    occupied = pairs // summed_occ
    slots, full_virtual, width = amplitudes.shape[1:]
    here = full_virtual // chips

    pieces = regroup(amplitudes, chips)
    moved = lax.all_to_all(pieces, "chip", split_axis=0, concat_axis=0, tiled=True)
    moved = moved.reshape(-1, width)
    flat = integrals.reshape(2, windows, summed_occ * integrals.shape[3], full_virtual)
    flat = pltpu.with_memory_space_constraint(flat, pltpu.HBM)
    across = lax.ppermute(moved, "core", SWAP)

    tables = pair_table.reshape(chips, 2, slots).transpose(1, 0, 2).reshape(2, 1, chips * slots)
    places = jnp.arange(full_virtual, dtype=jnp.int32)[:, None]
    natural_order = (kramers[None, :] == places).astype(BF16)
    chip_order = (kramers[None, :] == places % chips * here + places // chips).astype(BF16)

    mine, slabs, chooser = order(place, moved, tables, flat, occupied)
    matrices, to_send = first_window(mine, across, chooser, slabs, occupied)
    got = lax.ppermute(to_send, "vir", SWAP)
    kept = second_window(place, matrices, flat)
    own, mirror = combine(kept, got, natural_order, chip_order, chips)
    mirror = lax.all_to_all(mirror.reshape(chips, 8, -1), "chip", split_axis=0, concat_axis=0, tiled=True)
    keep, to_core, to_vir, to_both = subtract(place, own, mirror.reshape(chips * 8, -1))
    from_vir = lax.ppermute(to_vir, "vir", SWAP)
    from_both = lax.ppermute(to_both, ("core", "vir"), SWAP_BOTH)
    from_core = lax.ppermute(to_core, "core", SWAP)
    got_pieces = (keep, from_core, from_vir, from_both)
    out = finish(place, got_pieces)
    return out.reshape(2, windows, occupied, here // 2, width)


def solution(mesh):
    pair, vir = mesh.devices.shape
    split = Mesh(mesh.devices.reshape(pair // 2, 2, vir), ("chip", "core", "vir"))
    over_pair = ("chip", "core")
    placed = (P(None, over_pair, None, "vir"), P(None, None, None, "vir", None), P(), P())
    return jax.shard_map(
        body,
        mesh=split,
        in_specs=placed,
        out_specs=P(None, None, None, over_pair, "vir"),
        check_vma=False,
    )
```

```python
import functools

import jax
import jax.numpy as jnp
from jax import lax
from jax.experimental import pallas as pl
from jax.experimental.pallas import tpu as pltpu
from jax.sharding import Mesh
from jax.sharding import PartitionSpec as P

F32 = jnp.float32
BF16 = jnp.bfloat16
NT = (((1,), (1,)), ((), ()))
VMEM_LIMIT = 24 * 1024 * 1024
IN_VMEM = pl.BlockSpec(memory_space=pltpu.VMEM)
KS_A_BLOCK = 6
IN_HBM = pl.BlockSpec(memory_space=pl.ANY)
IN_SMEM = pl.BlockSpec(memory_space=pltpu.SMEM)
PARAMS = pltpu.CompilerParams(vmem_limit_bytes=VMEM_LIMIT)


def cost(flops, moved_bytes):
    return pl.CostEstimate(flops=int(flops), bytes_accessed=int(moved_bytes), transcendentals=0)


def regroup_kernel(src, dst, planes, sems):
    parts, slots = src.shape[:2]
    copies = [
        pltpu.make_async_copy(src.at[part, slot], planes.at[part, slot], sems.at[part, slot])
        for part in range(parts)
        for slot in range(slots)
    ]
    for copy in copies:
        copy.start()
    for part in range(parts):
        for slot in range(slots):
            copies[part * slots + slot].wait()
            dst[:, slot * parts + part] = planes[part, slot]


def regroup(amplitudes, chips):
    parts, slots, rows, width = amplitudes.shape
    here = rows // chips
    planes = amplitudes.reshape(parts, slots, chips, here, width)
    return pl.pallas_call(
        regroup_kernel,
        out_shape=jax.ShapeDtypeStruct((chips, parts * slots, here, width), amplitudes.dtype),
        in_specs=[IN_HBM],
        out_specs=IN_VMEM,
        scratch_shapes=[pltpu.VMEM(planes.shape, planes.dtype), pltpu.SemaphoreType.DMA((parts, slots))],
        compiler_params=PARAMS,
        name="regroup",
    )(pltpu.with_memory_space_constraint(planes, pltpu.HBM))


def slab_copies(place, turn, integrals, slabs, sems):
    vir, core = place[0] % 2, (place[0] // 2) % 2
    window = 2 * core + (1 - vir if turn == 0 else vir)
    return [pltpu.make_async_copy(integrals.at[part, window], slabs.at[part], sems.at[part]) for part in range(2)]


def spread_rows(moved, wide, slots_by):
    slots = slots_by.shape[0]
    width = moved.shape[1]
    rows = moved.shape[0] // slots
    pitch = slots + 1
    slots_a_step = 32

    def step(index, carry):
        at = index * slots_a_step
        values = moved[pl.ds(pl.multiple_of(at * rows, slots_a_step * rows), slots_a_step * rows), :].astype(F32)
        for slot in range(slots_a_step):
            wide[pl.ds(at + slot, rows, stride=pitch), :] = values[slot * rows : (slot + 1) * rows]
        return carry

    lax.fori_loop(0, slots // slots_a_step, step, 0)
    for row in range(rows):
        slots_by[:, row * width : (row + 1) * width] = wide[row * pitch : row * pitch + slots, :].astype(BF16)


def order_block(start, chooser, slots_by, matrices, mine, width, occupied):
    ordered = jnp.dot(
        chooser[start * occupied : (start + KS_A_BLOCK) * occupied, :], slots_by[...], preferred_element_type=F32
    ).astype(BF16)
    for k in range(KS_A_BLOCK):
        for row in range(slots_by.shape[1] // width):
            at = slice(row * occupied, (row + 1) * occupied)
            lanes = slice((start + k) * width, (start + k + 1) * width)
            block = ordered[k * occupied : (k + 1) * occupied, row * width : (row + 1) * width]
            matrices[at, lanes] = block if mine is None else mine[at, lanes] + block


def choose(chooser, table, occupied):
    pairs, slots = chooser.shape
    lanes = 128
    row = lax.broadcasted_iota(jnp.int32, (pairs, lanes), 0)
    wanted = row % occupied * (pairs // occupied) + row // occupied
    for start in range(0, slots, lanes):
        chooser[:, start : start + lanes] = (table[:, start : start + lanes] == wanted).astype(BF16)


def sort_table(table, tables, select, slots_a_chip):
    pairs = table.shape[1]
    slots = pairs // 2
    lanes = 128
    column = lax.broadcasted_iota(jnp.int32, (1, pairs), 1)
    core = (column >= slots).astype(jnp.int32)
    within = column - core * slots
    chip = within // slots_a_chip
    stored = within + (chip + core) * slots_a_chip
    row = lax.broadcasted_iota(jnp.int32, (pairs, lanes), 0)
    for start in range(0, pairs, lanes):
        select[:, start : start + lanes] = (row == stored[:, start : start + lanes]).astype(BF16)
    values = jnp.broadcast_to(table[...], (16, pairs))
    digit = lax.broadcasted_iota(jnp.int32, (16, pairs), 0)
    digits = jnp.where(digit == 0, values // 32, values % 32).astype(F32).astype(BF16)
    moved = jnp.dot(digits, select[...], preferred_element_type=F32)
    sorted_table = (moved[0:1] * 32 + moved[1:2]).astype(jnp.int32)
    tables[0] = sorted_table[:, :slots]
    tables[1] = sorted_table[:, slots:]


def order_kernel(
    place, moved, table, integrals, matrices, slabs, there, here, wide, slots_by, tables, select, sems, *, occupied, chips
):
    copies = slab_copies(place, 0, integrals, slabs, sems)
    for copy in copies:
        copy.start()
    core = (place[0] // 2) % 2
    sort_table(table, tables, select, here.shape[1] // chips)
    choose(here, tables[core], occupied)
    spread_rows(moved, wide, slots_by)
    for start in range(0, here.shape[0] // occupied, KS_A_BLOCK):
        order_block(start, here, slots_by, matrices, None, moved.shape[1], occupied)
    choose(there, tables[1 - core], occupied)
    for copy in copies:
        copy.wait()


def order(place, moved, table, integrals, occupied, chips):
    pairs = table.shape[1]
    slots = pairs // 2
    width = moved.shape[1]
    rows = moved.shape[0] // slots
    return pl.pallas_call(
        functools.partial(order_kernel, occupied=occupied, chips=chips),
        out_shape=(
            pltpu.VMEM((rows * occupied, pairs // occupied * width), BF16),
            pltpu.VMEM((2,) + integrals.shape[2:], BF16),
            pltpu.VMEM((pairs, slots), BF16),
        ),
        in_specs=[IN_SMEM, IN_VMEM, IN_VMEM, IN_HBM],
        out_specs=(IN_VMEM,) * 3,
        scratch_shapes=[
            pltpu.VMEM((pairs, slots), BF16),
            pltpu.VMEM(((slots + 1) * rows, width), F32),
            pltpu.VMEM((slots, rows * width), BF16),
            pltpu.VMEM((2, 1, slots), jnp.int32),
            pltpu.VMEM((pairs, pairs), BF16),
            pltpu.SemaphoreType.DMA((2,)),
        ],
        compiler_params=PARAMS,
        cost_estimate=cost(2 * pairs * slots * rows * width, integrals.size),
        name="order",
    )(place, moved, table, integrals)


def product_into(out, matrices, slabs, copies=()):
    half = matrices.shape[0] // 2
    for copy in copies[:1]:
        copy.wait()
    by_real = jnp.dot(matrices[...], slabs[0], preferred_element_type=F32)
    for copy in copies[1:]:
        copy.wait()
    by_imag = jnp.dot(matrices[...], slabs[1], preferred_element_type=F32)
    out[:half] = by_real[:half] - by_imag[half:]
    out[half:] = by_real[half:] + by_imag[:half]


def first_kernel(mine, moved, chooser, slabs, matrices, out, wide, slots_by, by_real, by_imag, *, occupied):
    half = matrices.shape[0] // 2
    width = moved.shape[1]
    slots = slots_by.shape[0]
    rows = moved.shape[0] // slots
    wide[...] = moved[...].astype(F32)
    for row in range(rows):
        slots_by[:, row * width : (row + 1) * width] = wide[pl.ds(row, slots, stride=rows), :].astype(BF16)
    summed_occ = chooser.shape[0] // occupied
    order_block(0, chooser, slots_by, matrices, mine, width, occupied)
    for start in range(0, summed_occ, KS_A_BLOCK):
        if start + KS_A_BLOCK < summed_occ:
            order_block(start + KS_A_BLOCK, chooser, slots_by, matrices, mine, width, occupied)
        lanes = slice(start * width, (start + KS_A_BLOCK) * width)
        for part, total in enumerate((by_real, by_imag)):
            product = jnp.dot(matrices[:, lanes], slabs[part, lanes], preferred_element_type=F32)
            total[...] = product if start == 0 else total[...] + product
    out[:half] = by_real[:half] - by_imag[half:]
    out[half:] = by_real[half:] + by_imag[:half]


def first_window(mine, moved, chooser, slabs, occupied):
    width = moved.shape[1]
    slots = chooser.shape[1]
    rows = moved.shape[0] // slots
    full_virtual = slabs.shape[-1]
    return pl.pallas_call(
        functools.partial(first_kernel, occupied=occupied),
        out_shape=(
            jax.ShapeDtypeStruct(mine.shape, BF16),
            jax.ShapeDtypeStruct((mine.shape[0], full_virtual), F32),
        ),
        in_specs=[IN_VMEM] * 4,
        out_specs=(IN_VMEM,) * 2,
        scratch_shapes=[
            pltpu.VMEM(moved.shape, F32),
            pltpu.VMEM((slots, rows * width), BF16),
            pltpu.VMEM((mine.shape[0], full_virtual), F32),
            pltpu.VMEM((mine.shape[0], full_virtual), F32),
        ],
        compiler_params=PARAMS,
        cost_estimate=cost(4 * mine.size * full_virtual, 4 * mine.size),
        name="first_window",
    )(mine, moved, chooser, pltpu.with_memory_space_constraint(slabs, pltpu.VMEM))


def second_kernel(place, matrices, integrals, out, slabs, sems):
    copies = slab_copies(place, 1, integrals, slabs, sems)
    for copy in copies:
        copy.start()
    product_into(out, matrices, slabs, copies)


def second_window(place, matrices, integrals):
    depth, full_virtual = integrals.shape[2:]
    return pl.pallas_call(
        second_kernel,
        out_shape=jax.ShapeDtypeStruct((matrices.shape[0], full_virtual), F32),
        in_specs=[IN_SMEM, IN_VMEM, IN_HBM],
        out_specs=IN_VMEM,
        scratch_shapes=[pltpu.VMEM((2, depth, full_virtual), BF16), pltpu.SemaphoreType.DMA((2,))],
        compiler_params=PARAMS,
        cost_estimate=cost(4 * matrices.size * full_virtual, 4 * matrices.size),
        name="second_window",
    )(place, matrices, integrals)


def chosen(values, order_by):
    high = values.astype(BF16)
    rest = values - high.astype(F32)
    middle = rest.astype(BF16)
    low = (rest - middle.astype(F32)).astype(BF16)
    total = lax.dot_general(low, order_by, NT, preferred_element_type=F32)
    total += lax.dot_general(middle, order_by, NT, preferred_element_type=F32)
    return total + lax.dot_general(high, order_by, NT, preferred_element_type=F32)


def combine_kernel(kept, got, natural_order, chip_order, own, mirror):
    full_virtual = kept.shape[1]
    rows = kept.shape[0] // 2
    chips = mirror.shape[0] // 8
    here = full_virtual // chips
    occupied = rows // here
    lane = lax.broadcasted_iota(jnp.int32, (occupied, 2 * chips), 1)
    values = kept[...] + got[...]
    by_chip = chosen(values, chip_order[...])
    own[...] = chosen(values, natural_order[...])
    for part in range(2):
        for row in range(0, here, 2):
            at = part * rows + row * occupied
            blocks = []
            for other in range(0, here, 2):
                lanes = slice(other * chips, (other + 2) * chips)
                low = by_chip[at : at + occupied, lanes]
                high = by_chip[at + occupied : at + 2 * occupied, lanes]
                blocks.append(jnp.where(lane < chips, low, pltpu.roll(high, chips, 1)))
                blocks.append(jnp.where(lane < chips, pltpu.roll(low, chips, 1), high))
            turned = jnp.concatenate(blocks, axis=0).T
            mirror[pl.ds(2 * row + part, chips, stride=8), :] = turned[:chips]
            mirror[pl.ds(2 * (row + 1) + part, chips, stride=8), :] = turned[chips:]


def combine(kept, got, natural_order, chip_order, chips):
    return pl.pallas_call(
        combine_kernel,
        out_shape=(jax.ShapeDtypeStruct(kept.shape, F32), jax.ShapeDtypeStruct((chips * 8, kept.shape[0] // 2), F32)),
        compiler_params=PARAMS,
        name="combine",
    )(kept, got, natural_order, chip_order)


def subtract_kernel(place, own, mirror, keep, to_core, to_vir, to_both, block):
    vir, core = place[0] % 2, (place[0] // 2) % 2
    here = 2 * block.shape[1]
    rows, full_virtual = own.shape[0] // 2, own.shape[1]
    occupied = rows // here
    half = full_virtual // 2
    lanes = (slice(0, half), slice(half, full_virtual))
    for part in range(2):
        values = own[part * rows : (part + 1) * rows] - mirror[pl.ds(part, full_virtual, stride=2), :].T
        for row in range(here):
            for side in range(2):
                block[part, row // 2, side, pl.ds(row % 2, occupied, stride=2), :] = values[
                    row * occupied : (row + 1) * occupied, lanes[side]
                ]
    for target, to_side, to_half in (
        (keep, core, vir),
        (to_core, 1 - core, vir),
        (to_vir, core, 1 - vir),
        (to_both, 1 - core, 1 - vir),
    ):
        for part in range(2):
            target[part] = block[part, to_side, to_half].astype(BF16)


def subtract(place, own, mirror):
    rows, full_virtual = own.shape[0] // 2, own.shape[1]
    piece = jax.ShapeDtypeStruct((2, rows // 2, full_virtual // 2), BF16)
    return pl.pallas_call(
        subtract_kernel,
        out_shape=(piece,) * 4,
        in_specs=[IN_SMEM, IN_VMEM, IN_VMEM],
        out_specs=(IN_VMEM,) * 4,
        scratch_shapes=[pltpu.VMEM((2, 2, 2, rows // 2, full_virtual // 2), F32)],
        compiler_params=PARAMS,
        name="subtract",
    )(place, own, mirror)


def finish_kernel(place, keep, from_core, from_vir, from_both, out):
    vir, core = place[0] % 2, (place[0] // 2) % 2
    out[:, 2 * core + vir] = keep[...]
    out[:, 2 * (1 - core) + vir] = from_core[...]
    out[:, 2 * core + 1 - vir] = from_vir[...]
    out[:, 2 * (1 - core) + 1 - vir] = from_both[...]


def finish(place, pieces):
    _, rows, width = pieces[0].shape
    return pl.pallas_call(
        finish_kernel,
        out_shape=jax.ShapeDtypeStruct((2, 4, rows, width), BF16),
        in_specs=[IN_SMEM] + [IN_VMEM] * 4,
        out_specs=IN_VMEM,
        compiler_params=PARAMS,
        name="finish",
    )(place, *pieces)


SWAP = [(0, 1), (1, 0)]
SWAP_BOTH = [(0, 3), (1, 2), (2, 1), (3, 0)]


def body(amplitudes, integrals, pair_table, kramers):
    chips = lax.axis_size("chip")
    place = lax.axis_index(("chip", "core", "vir")).astype(jnp.int32).reshape(1)
    windows, summed_occ = integrals.shape[1:3]
    pairs = pair_table.shape[0]
    occupied = pairs // summed_occ
    slots, full_virtual, width = amplitudes.shape[1:]
    here = full_virtual // chips

    pieces = regroup(amplitudes, chips)
    moved = lax.all_to_all(pieces, "chip", split_axis=0, concat_axis=0, tiled=True)
    moved = moved.reshape(-1, width)
    flat = integrals.reshape(2, windows, summed_occ * integrals.shape[3], full_virtual)
    flat = pltpu.with_memory_space_constraint(flat, pltpu.HBM)
    across = lax.ppermute(moved, "core", SWAP)

    places = jnp.arange(full_virtual, dtype=jnp.int32)[:, None]
    natural_order = (kramers[None, :] == places).astype(BF16)
    chip_order = (kramers[None, :] == places % chips * here + places // chips).astype(BF16)

    mine, slabs, chooser = order(place, moved, pair_table.reshape(1, pairs), flat, occupied, chips)
    matrices, to_send = first_window(mine, across, chooser, slabs, occupied)
    got = lax.ppermute(to_send, "vir", SWAP)
    kept = second_window(place, matrices, flat)
    own, mirror = combine(kept, got, natural_order, chip_order, chips)
    mirror = lax.all_to_all(mirror.reshape(chips, 8, -1), "chip", split_axis=0, concat_axis=0, tiled=True)
    keep, to_core, to_vir, to_both = subtract(place, own, mirror.reshape(chips * 8, -1))
    from_vir = lax.ppermute(to_vir, "vir", SWAP)
    from_both = lax.ppermute(to_both, ("core", "vir"), SWAP_BOTH)
    from_core = lax.ppermute(to_core, "core", SWAP)
    got_pieces = (keep, from_core, from_vir, from_both)
    out = finish(place, got_pieces)
    return out.reshape(2, windows, occupied, here // 2, width)


def solution(mesh):
    pair, vir = mesh.devices.shape
    split = Mesh(mesh.devices.reshape(pair // 2, 2, vir), ("chip", "core", "vir"))
    over_pair = ("chip", "core")
    placed = (P(None, over_pair, None, "vir"), P(None, None, None, "vir", None), P(), P())
    return jax.shard_map(
        body,
        mesh=split,
        in_specs=placed,
        out_specs=P(None, None, None, over_pair, "vir"),
        check_vma=False,
    )
```

```python
import functools

import jax
import jax.numpy as jnp
from jax import lax
from jax.experimental import pallas as pl
from jax.experimental.pallas import tpu as pltpu
from jax.sharding import Mesh
from jax.sharding import PartitionSpec as P

F32 = jnp.float32
BF16 = jnp.bfloat16
NT = (((1,), (1,)), ((), ()))
VMEM_LIMIT = 24 * 1024 * 1024
IN_VMEM = pl.BlockSpec(memory_space=pltpu.VMEM)
KS_A_BLOCK = 8
IN_HBM = pl.BlockSpec(memory_space=pl.ANY)
IN_SMEM = pl.BlockSpec(memory_space=pltpu.SMEM)
PARAMS = pltpu.CompilerParams(vmem_limit_bytes=VMEM_LIMIT)


def cost(flops, moved_bytes):
    return pl.CostEstimate(flops=int(flops), bytes_accessed=int(moved_bytes), transcendentals=0)


def regroup_kernel(src, dst, planes, sems):
    parts, slots = src.shape[:2]
    copies = [
        pltpu.make_async_copy(src.at[part, slot], planes.at[part, slot], sems.at[part, slot])
        for part in range(parts)
        for slot in range(slots)
    ]
    for copy in copies:
        copy.start()
    for part in range(parts):
        for slot in range(slots):
            copies[part * slots + slot].wait()
            dst[:, slot * parts + part] = planes[part, slot]


def regroup(amplitudes, chips):
    parts, slots, rows, width = amplitudes.shape
    here = rows // chips
    planes = amplitudes.reshape(parts, slots, chips, here, width)
    return pl.pallas_call(
        regroup_kernel,
        out_shape=jax.ShapeDtypeStruct((chips, parts * slots, here, width), amplitudes.dtype),
        in_specs=[IN_HBM],
        out_specs=IN_VMEM,
        scratch_shapes=[pltpu.VMEM(planes.shape, planes.dtype), pltpu.SemaphoreType.DMA((parts, slots))],
        compiler_params=PARAMS,
        name="regroup",
    )(pltpu.with_memory_space_constraint(planes, pltpu.HBM))


def slab_copies(place, turn, integrals, slabs, sems):
    vir, core = place[0] % 2, (place[0] // 2) % 2
    window = 2 * core + (1 - vir if turn == 0 else vir)
    return [pltpu.make_async_copy(integrals.at[part, window], slabs.at[part], sems.at[part]) for part in range(2)]


def spread_rows(moved, wide, slots_by):
    slots = slots_by.shape[0]
    width = moved.shape[1]
    rows = moved.shape[0] // slots
    pitch = slots + 1
    slots_a_step = 32

    def step(index, carry):
        at = index * slots_a_step
        values = moved[pl.ds(pl.multiple_of(at * rows, slots_a_step * rows), slots_a_step * rows), :].astype(F32)
        for slot in range(slots_a_step):
            wide[pl.ds(at + slot, rows, stride=pitch), :] = values[slot * rows : (slot + 1) * rows]
        return carry

    lax.fori_loop(0, slots // slots_a_step, step, 0)
    for row in range(rows):
        slots_by[:, row * width : (row + 1) * width] = wide[row * pitch : row * pitch + slots, :].astype(BF16)


def order_block(start, chooser, slots_by, matrices, mine, width, occupied):
    ordered = jnp.dot(
        chooser[start * occupied : (start + KS_A_BLOCK) * occupied, :], slots_by[...], preferred_element_type=F32
    ).astype(BF16)
    for k in range(KS_A_BLOCK):
        for row in range(slots_by.shape[1] // width):
            at = slice(row * occupied, (row + 1) * occupied)
            lanes = slice((start + k) * width, (start + k + 1) * width)
            block = ordered[k * occupied : (k + 1) * occupied, row * width : (row + 1) * width]
            matrices[at, lanes] = block if mine is None else mine[at, lanes] + block


def choose(chooser, table, occupied):
    pairs, slots = chooser.shape
    lanes = 128
    row = lax.broadcasted_iota(jnp.int32, (pairs, lanes), 0)
    wanted = row % occupied * (pairs // occupied) + row // occupied
    for start in range(0, slots, lanes):
        chooser[:, start : start + lanes] = (table[:, start : start + lanes] == wanted).astype(BF16)


def order_kernel(place, moved, tables, integrals, matrices, slabs, there, here, wide, slots_by, sems, *, occupied):
    copies = slab_copies(place, 0, integrals, slabs, sems)
    for copy in copies:
        copy.start()
    core = (place[0] // 2) % 2
    choose(here, tables[core], occupied)
    spread_rows(moved, wide, slots_by)
    for start in range(0, here.shape[0] // occupied, KS_A_BLOCK):
        order_block(start, here, slots_by, matrices, None, moved.shape[1], occupied)
    choose(there, tables[1 - core], occupied)
    for copy in copies:
        copy.wait()


def order(place, moved, tables, integrals, occupied):
    slots = tables.shape[2]
    pairs = 2 * slots
    width = moved.shape[1]
    rows = moved.shape[0] // slots
    return pl.pallas_call(
        functools.partial(order_kernel, occupied=occupied),
        out_shape=(
            pltpu.VMEM((rows * occupied, pairs // occupied * width), BF16),
            pltpu.VMEM((2,) + integrals.shape[2:], BF16),
            pltpu.VMEM((pairs, slots), BF16),
        ),
        in_specs=[IN_SMEM, IN_VMEM, IN_VMEM, IN_HBM],
        out_specs=(IN_VMEM,) * 3,
        scratch_shapes=[
            pltpu.VMEM((pairs, slots), BF16),
            pltpu.VMEM(((slots + 1) * rows, width), F32),
            pltpu.VMEM((slots, rows * width), BF16),
            pltpu.SemaphoreType.DMA((2,)),
        ],
        compiler_params=PARAMS,
        cost_estimate=cost(2 * pairs * slots * rows * width, integrals.size),
        name="order",
    )(place, moved, tables, integrals)


def product_into(out, matrices, slabs, copies=()):
    half = matrices.shape[0] // 2
    for copy in copies[:1]:
        copy.wait()
    by_real = jnp.dot(matrices[...], slabs[0], preferred_element_type=F32)
    for copy in copies[1:]:
        copy.wait()
    by_imag = jnp.dot(matrices[...], slabs[1], preferred_element_type=F32)
    out[:half] = by_real[:half] - by_imag[half:]
    out[half:] = by_real[half:] + by_imag[:half]


def first_kernel(mine, moved, chooser, slabs, matrices, out, wide, slots_by, by_real, by_imag, *, occupied):
    half = matrices.shape[0] // 2
    width = moved.shape[1]
    spread_rows(moved, wide, slots_by)
    summed_occ = chooser.shape[0] // occupied
    order_block(0, chooser, slots_by, matrices, mine, width, occupied)
    for start in range(0, summed_occ, KS_A_BLOCK):
        if start + KS_A_BLOCK < summed_occ:
            order_block(start + KS_A_BLOCK, chooser, slots_by, matrices, mine, width, occupied)
        lanes = slice(start * width, (start + KS_A_BLOCK) * width)
        for part, total in enumerate((by_real, by_imag)):
            product = jnp.dot(matrices[:, lanes], slabs[part, lanes], preferred_element_type=F32)
            total[...] = product if start == 0 else total[...] + product
    out[:half] = by_real[:half] - by_imag[half:]
    out[half:] = by_real[half:] + by_imag[:half]


def first_window(mine, moved, chooser, slabs, occupied):
    width = moved.shape[1]
    slots = chooser.shape[1]
    rows = moved.shape[0] // slots
    full_virtual = slabs.shape[-1]
    return pl.pallas_call(
        functools.partial(first_kernel, occupied=occupied),
        out_shape=(
            jax.ShapeDtypeStruct(mine.shape, BF16),
            jax.ShapeDtypeStruct((mine.shape[0], full_virtual), F32),
        ),
        in_specs=[IN_VMEM] * 4,
        out_specs=(IN_VMEM,) * 2,
        scratch_shapes=[
            pltpu.VMEM(((slots + 1) * rows, width), F32),
            pltpu.VMEM((slots, rows * width), BF16),
            pltpu.VMEM((mine.shape[0], full_virtual), F32),
            pltpu.VMEM((mine.shape[0], full_virtual), F32),
        ],
        compiler_params=PARAMS,
        cost_estimate=cost(4 * mine.size * full_virtual, 4 * mine.size),
        name="first_window",
    )(mine, moved, chooser, pltpu.with_memory_space_constraint(slabs, pltpu.VMEM))


def second_kernel(place, matrices, integrals, out, slabs, sems):
    copies = slab_copies(place, 1, integrals, slabs, sems)
    for copy in copies:
        copy.start()
    product_into(out, matrices, slabs, copies)


def second_window(place, matrices, integrals):
    depth, full_virtual = integrals.shape[2:]
    return pl.pallas_call(
        second_kernel,
        out_shape=jax.ShapeDtypeStruct((matrices.shape[0], full_virtual), F32),
        in_specs=[IN_SMEM, IN_VMEM, IN_HBM],
        out_specs=IN_VMEM,
        scratch_shapes=[pltpu.VMEM((2, depth, full_virtual), BF16), pltpu.SemaphoreType.DMA((2,))],
        compiler_params=PARAMS,
        cost_estimate=cost(4 * matrices.size * full_virtual, 4 * matrices.size),
        name="second_window",
    )(place, matrices, integrals)


def chosen(values, order_by):
    high = values.astype(BF16)
    rest = values - high.astype(F32)
    middle = rest.astype(BF16)
    low = (rest - middle.astype(F32)).astype(BF16)
    total = lax.dot_general(low, order_by, NT, preferred_element_type=F32)
    total += lax.dot_general(middle, order_by, NT, preferred_element_type=F32)
    return total + lax.dot_general(high, order_by, NT, preferred_element_type=F32)


def combine_kernel(kept, got, chip_order, own, mirror):
    full_virtual = kept.shape[1]
    rows = kept.shape[0] // 2
    chips = mirror.shape[0] // 8
    here = full_virtual // chips
    occupied = rows // here
    lane = lax.broadcasted_iota(jnp.int32, (occupied, 2 * chips), 1)
    values = kept[...] + got[...]
    by_chip = chosen(values, chip_order[...])
    own[...] = by_chip
    for part in range(2):
        for row in range(0, here, 2):
            at = part * rows + row * occupied
            blocks = []
            for other in range(0, here, 2):
                lanes = slice(other * chips, (other + 2) * chips)
                low = by_chip[at : at + occupied, lanes]
                high = by_chip[at + occupied : at + 2 * occupied, lanes]
                blocks.append(jnp.where(lane < chips, low, pltpu.roll(high, chips, 1)))
                blocks.append(jnp.where(lane < chips, pltpu.roll(low, chips, 1), high))
            turned = jnp.concatenate(blocks, axis=0).T
            mirror[pl.ds(2 * row + part, chips, stride=8), :] = turned[:chips]
            mirror[pl.ds(2 * (row + 1) + part, chips, stride=8), :] = turned[chips:]


def combine(kept, got, chip_order, chips):
    return pl.pallas_call(
        combine_kernel,
        out_shape=(jax.ShapeDtypeStruct(kept.shape, F32), jax.ShapeDtypeStruct((chips * 8, kept.shape[0] // 2), F32)),
        compiler_params=PARAMS,
        name="combine",
    )(kept, got, chip_order)


def subtract_kernel(place, own, mirror, to_natural, keep, to_core, to_vir, to_both, block):
    vir, core = place[0] % 2, (place[0] // 2) % 2
    here = 2 * block.shape[1]
    rows, full_virtual = own.shape[0] // 2, own.shape[1]
    occupied = rows // here
    half = full_virtual // 2
    lanes = (slice(0, half), slice(half, full_virtual))
    chips = mirror.shape[0] // 8
    for part in range(2):
        turned = jnp.concatenate([mirror[pl.ds(2 * row + part, chips, stride=8), :] for row in range(here)], axis=0).T
        values = (own[part * rows : (part + 1) * rows] - turned).astype(BF16)
        values = jnp.dot(values, to_natural[...], preferred_element_type=F32)
        for row in range(here):
            for side in range(2):
                block[part, row // 2, side, pl.ds(row % 2, occupied, stride=2), :] = values[
                    row * occupied : (row + 1) * occupied, lanes[side]
                ]
    for target, to_side, to_half in (
        (keep, core, vir),
        (to_core, 1 - core, vir),
        (to_vir, core, 1 - vir),
        (to_both, 1 - core, 1 - vir),
    ):
        for part in range(2):
            target[part] = block[part, to_side, to_half].astype(BF16)


def subtract(place, own, mirror, to_natural):
    rows, full_virtual = own.shape[0] // 2, own.shape[1]
    piece = jax.ShapeDtypeStruct((2, rows // 2, full_virtual // 2), BF16)
    return pl.pallas_call(
        subtract_kernel,
        out_shape=(piece,) * 4,
        in_specs=[IN_SMEM] + [IN_VMEM] * 3,
        out_specs=(IN_VMEM,) * 4,
        scratch_shapes=[pltpu.VMEM((2, 2, 2, rows // 2, full_virtual // 2), F32)],
        compiler_params=PARAMS,
        name="subtract",
    )(place, own, mirror, to_natural)


def finish_kernel(place, keep, from_core, from_vir, from_both, out):
    vir, core = place[0] % 2, (place[0] // 2) % 2
    out[:, 2 * core + vir] = keep[...]
    out[:, 2 * (1 - core) + vir] = from_core[...]
    out[:, 2 * core + 1 - vir] = from_vir[...]
    out[:, 2 * (1 - core) + 1 - vir] = from_both[...]


def finish(place, pieces):
    _, rows, width = pieces[0].shape
    return pl.pallas_call(
        finish_kernel,
        out_shape=jax.ShapeDtypeStruct((2, 4, rows, width), BF16),
        in_specs=[IN_SMEM] + [IN_VMEM] * 4,
        out_specs=IN_VMEM,
        compiler_params=PARAMS,
        name="finish",
    )(place, *pieces)


SWAP = [(0, 1), (1, 0)]
SWAP_BOTH = [(0, 3), (1, 2), (2, 1), (3, 0)]


def body(amplitudes, integrals, pair_table, kramers):
    chips = lax.axis_size("chip")
    place = lax.axis_index(("chip", "core", "vir")).astype(jnp.int32).reshape(1)
    windows, summed_occ = integrals.shape[1:3]
    pairs = pair_table.shape[0]
    occupied = pairs // summed_occ
    slots, full_virtual, width = amplitudes.shape[1:]
    here = full_virtual // chips

    pieces = regroup(amplitudes, chips)
    moved = lax.all_to_all(pieces, "chip", split_axis=0, concat_axis=0, tiled=True)
    moved = moved.reshape(-1, width)
    flat = integrals.reshape(2, windows, summed_occ * integrals.shape[3], full_virtual)
    flat = pltpu.with_memory_space_constraint(flat, pltpu.HBM)
    across = lax.ppermute(moved, "core", SWAP)

    tables = pair_table.reshape(chips, 2, slots).transpose(1, 0, 2).reshape(2, 1, chips * slots)
    places = jnp.arange(full_virtual, dtype=jnp.int32)[:, None]
    to_natural = (places % chips * here + places // chips == places.T).astype(BF16)
    chip_order = (kramers[None, :] == places % chips * here + places // chips).astype(BF16)

    mine, slabs, chooser = order(place, moved, tables, flat, occupied)
    matrices, to_send = first_window(mine, across, chooser, slabs, occupied)
    got = lax.ppermute(to_send, "vir", SWAP)
    kept = second_window(place, matrices, flat)
    own, mirror = combine(kept, got, chip_order, chips)
    mirror = lax.all_to_all(mirror.reshape(chips, 8, -1), "chip", split_axis=0, concat_axis=0, tiled=True)
    keep, to_core, to_vir, to_both = subtract(place, own, mirror.reshape(chips * 8, -1), to_natural)
    from_vir = lax.ppermute(to_vir, "vir", SWAP)
    from_both = lax.ppermute(to_both, ("core", "vir"), SWAP_BOTH)
    from_core = lax.ppermute(to_core, "core", SWAP)
    got_pieces = (keep, from_core, from_vir, from_both)
    out = finish(place, got_pieces)
    return out.reshape(2, windows, occupied, here // 2, width)


def solution(mesh):
    pair, vir = mesh.devices.shape
    split = Mesh(mesh.devices.reshape(pair // 2, 2, vir), ("chip", "core", "vir"))
    over_pair = ("chip", "core")
    placed = (P(None, over_pair, None, "vir"), P(None, None, None, "vir", None), P(), P())
    return jax.shard_map(
        body,
        mesh=split,
        in_specs=placed,
        out_specs=P(None, None, None, over_pair, "vir"),
        check_vma=False,
    )
```

```python
import functools

import jax
import jax.numpy as jnp
from jax import lax
from jax.experimental import pallas as pl
from jax.experimental.pallas import tpu as pltpu
from jax.sharding import Mesh
from jax.sharding import PartitionSpec as P

F32 = jnp.float32
BF16 = jnp.bfloat16
NT = (((1,), (1,)), ((), ()))
VMEM_LIMIT = 24 * 1024 * 1024
IN_VMEM = pl.BlockSpec(memory_space=pltpu.VMEM)
KS_A_BLOCK = 8
IN_HBM = pl.BlockSpec(memory_space=pl.ANY)
IN_SMEM = pl.BlockSpec(memory_space=pltpu.SMEM)
PARAMS = pltpu.CompilerParams(vmem_limit_bytes=VMEM_LIMIT)


def cost(flops, moved_bytes):
    return pl.CostEstimate(flops=int(flops), bytes_accessed=int(moved_bytes), transcendentals=0)


def regroup_kernel(src, dst, planes, sems):
    parts, slots = src.shape[:2]
    copies = [
        pltpu.make_async_copy(src.at[part, slot], planes.at[part, slot], sems.at[part, slot])
        for part in range(parts)
        for slot in range(slots)
    ]
    for copy in copies:
        copy.start()
    for part in range(parts):
        for slot in range(slots):
            copies[part * slots + slot].wait()
            dst[:, slot * parts + part] = planes[part, slot]


def regroup(amplitudes, chips):
    parts, slots, rows, width = amplitudes.shape
    here = rows // chips
    planes = amplitudes.reshape(parts, slots, chips, here, width)
    return pl.pallas_call(
        regroup_kernel,
        out_shape=jax.ShapeDtypeStruct((chips, parts * slots, here, width), amplitudes.dtype),
        in_specs=[IN_HBM],
        out_specs=IN_VMEM,
        scratch_shapes=[pltpu.VMEM(planes.shape, planes.dtype), pltpu.SemaphoreType.DMA((parts, slots))],
        compiler_params=PARAMS,
        name="regroup",
    )(pltpu.with_memory_space_constraint(planes, pltpu.HBM))


def slab_copies(place, turn, integrals, slabs, sems):
    vir, core = place[0] % 2, (place[0] // 2) % 2
    window = 2 * core + (1 - vir if turn == 0 else vir)
    return [pltpu.make_async_copy(integrals.at[part, window], slabs.at[part], sems.at[part]) for part in range(2)]


def spread_rows(moved, wide, slots_by):
    slots = slots_by.shape[0]
    width = moved.shape[1]
    rows = moved.shape[0] // slots
    pitch = slots + 1
    slots_a_step = 32

    def step(index, carry):
        at = index * slots_a_step
        values = moved[pl.ds(pl.multiple_of(at * rows, slots_a_step * rows), slots_a_step * rows), :].astype(F32)
        for slot in range(slots_a_step):
            wide[pl.ds(at + slot, rows, stride=pitch), :] = values[slot * rows : (slot + 1) * rows]
        return carry

    lax.fori_loop(0, slots // slots_a_step, step, 0)
    for row in range(rows):
        slots_by[:, row * width : (row + 1) * width] = wide[row * pitch : row * pitch + slots, :].astype(BF16)


def order_block(start, chooser, slots_by, matrices, mine, width, occupied):
    ordered = jnp.dot(
        chooser[start * occupied : (start + KS_A_BLOCK) * occupied, :], slots_by[...], preferred_element_type=F32
    ).astype(BF16)
    for k in range(KS_A_BLOCK):
        for row in range(slots_by.shape[1] // width):
            at = slice(row * occupied, (row + 1) * occupied)
            lanes = slice((start + k) * width, (start + k + 1) * width)
            block = ordered[k * occupied : (k + 1) * occupied, row * width : (row + 1) * width]
            matrices[at, lanes] = block if mine is None else mine[at, lanes] + block


def choose(chooser, table, occupied):
    pairs, slots = chooser.shape
    lanes = 128
    row = lax.broadcasted_iota(jnp.int32, (pairs, lanes), 0)
    wanted = row % occupied * (pairs // occupied) + row // occupied
    for start in range(0, slots, lanes):
        chooser[:, start : start + lanes] = (table[:, start : start + lanes] == wanted).astype(BF16)


def order_kernel(place, moved, tables, integrals, matrices, slabs, there, here, wide, slots_by, sems, *, occupied):
    copies = slab_copies(place, 0, integrals, slabs, sems)
    for copy in copies:
        copy.start()
    core = (place[0] // 2) % 2
    choose(here, tables[core], occupied)
    spread_rows(moved, wide, slots_by)
    for start in range(0, here.shape[0] // occupied, KS_A_BLOCK):
        order_block(start, here, slots_by, matrices, None, moved.shape[1], occupied)
    choose(there, tables[1 - core], occupied)
    for copy in copies:
        copy.wait()


def order(place, moved, tables, integrals, occupied):
    slots = tables.shape[2]
    pairs = 2 * slots
    width = moved.shape[1]
    rows = moved.shape[0] // slots
    return pl.pallas_call(
        functools.partial(order_kernel, occupied=occupied),
        out_shape=(
            pltpu.VMEM((rows * occupied, pairs // occupied * width), BF16),
            pltpu.VMEM((2,) + integrals.shape[2:], BF16),
            pltpu.VMEM((pairs, slots), BF16),
        ),
        in_specs=[IN_SMEM, IN_VMEM, IN_VMEM, IN_HBM],
        out_specs=(IN_VMEM,) * 3,
        scratch_shapes=[
            pltpu.VMEM((pairs, slots), BF16),
            pltpu.VMEM(((slots + 1) * rows, width), F32),
            pltpu.VMEM((slots, rows * width), BF16),
            pltpu.SemaphoreType.DMA((2,)),
        ],
        compiler_params=PARAMS,
        cost_estimate=cost(2 * pairs * slots * rows * width, integrals.size),
        name="order",
    )(place, moved, tables, integrals)


def product_into(out, matrices, slabs, copies=()):
    half = matrices.shape[0] // 2
    for copy in copies[:1]:
        copy.wait()
    by_real = jnp.dot(matrices[...], slabs[0], preferred_element_type=F32)
    for copy in copies[1:]:
        copy.wait()
    by_imag = jnp.dot(matrices[...], slabs[1], preferred_element_type=F32)
    out[:half] = by_real[:half] - by_imag[half:]
    out[half:] = by_real[half:] + by_imag[:half]


def first_kernel(mine, moved, chooser, slabs, matrices, real, imag, wide, slots_by, by_real, by_imag, *, occupied):
    half = matrices.shape[0] // 2
    width = moved.shape[1]
    spread_rows(moved, wide, slots_by)
    summed_occ = chooser.shape[0] // occupied
    order_block(0, chooser, slots_by, matrices, mine, width, occupied)
    for start in range(0, summed_occ, KS_A_BLOCK):
        if start + KS_A_BLOCK < summed_occ:
            order_block(start + KS_A_BLOCK, chooser, slots_by, matrices, mine, width, occupied)
        lanes = slice(start * width, (start + KS_A_BLOCK) * width)
        for part, total in enumerate((by_real, by_imag)):
            product = jnp.dot(matrices[:, lanes], slabs[part, lanes], preferred_element_type=F32)
            total[...] = product if start == 0 else total[...] + product
    real[...] = by_real[:half] - by_imag[half:]
    imag[...] = by_real[half:] + by_imag[:half]


def first_window(mine, moved, chooser, slabs, occupied):
    width = moved.shape[1]
    slots = chooser.shape[1]
    rows = moved.shape[0] // slots
    full_virtual = slabs.shape[-1]
    return pl.pallas_call(
        functools.partial(first_kernel, occupied=occupied),
        out_shape=(
            jax.ShapeDtypeStruct(mine.shape, BF16),
            jax.ShapeDtypeStruct((mine.shape[0] // 2, full_virtual), F32),
            jax.ShapeDtypeStruct((mine.shape[0] // 2, full_virtual), F32),
        ),
        in_specs=[IN_VMEM] * 4,
        out_specs=(IN_VMEM,) * 3,
        scratch_shapes=[
            pltpu.VMEM(((slots + 1) * rows, width), F32),
            pltpu.VMEM((slots, rows * width), BF16),
            pltpu.VMEM((mine.shape[0], full_virtual), F32),
            pltpu.VMEM((mine.shape[0], full_virtual), F32),
        ],
        compiler_params=PARAMS,
        cost_estimate=cost(4 * mine.size * full_virtual, 4 * mine.size),
        name="first_window",
    )(mine, moved, chooser, pltpu.with_memory_space_constraint(slabs, pltpu.VMEM))


def second_kernel(place, matrices, integrals, out, slabs, sems):
    copies = slab_copies(place, 1, integrals, slabs, sems)
    for copy in copies:
        copy.start()
    product_into(out, matrices, slabs, copies)


def second_window(place, matrices, integrals):
    depth, full_virtual = integrals.shape[2:]
    return pl.pallas_call(
        second_kernel,
        out_shape=jax.ShapeDtypeStruct((matrices.shape[0], full_virtual), F32),
        in_specs=[IN_SMEM, IN_VMEM, IN_HBM],
        out_specs=IN_VMEM,
        scratch_shapes=[pltpu.VMEM((2, depth, full_virtual), BF16), pltpu.SemaphoreType.DMA((2,))],
        compiler_params=PARAMS,
        cost_estimate=cost(4 * matrices.size * full_virtual, 4 * matrices.size),
        name="second_window",
    )(place, matrices, integrals)


def chosen(values, order_by):
    high = values.astype(BF16)
    rest = values - high.astype(F32)
    middle = rest.astype(BF16)
    low = (rest - middle.astype(F32)).astype(BF16)
    total = lax.dot_general(low, order_by, NT, preferred_element_type=F32)
    total += lax.dot_general(middle, order_by, NT, preferred_element_type=F32)
    return total + lax.dot_general(high, order_by, NT, preferred_element_type=F32)


def combine_kernel(kept, got, natural_order, chip_order, *refs, part):
    own, mirror = refs[-2:]
    full_virtual = kept.shape[1]
    rows = kept.shape[0] // 2
    chips = full_virtual // 4
    here = full_virtual // chips
    occupied = rows // here
    lane = lax.broadcasted_iota(jnp.int32, (occupied, 2 * chips), 1)
    values = kept[part * rows : (part + 1) * rows] + got[...]
    by_chip = chosen(values, chip_order[...])
    own[...] = chosen(values, natural_order[...])
    if part == 1:
        for row in range(here):
            mirror[pl.ds(2 * row, chips, stride=8), :] = refs[0][pl.ds(row, chips, stride=4), :]
    for row in range(0, here, 2):
        at = row * occupied
        blocks = []
        for other in range(0, here, 2):
            lanes = slice(other * chips, (other + 2) * chips)
            low = by_chip[at : at + occupied, lanes]
            high = by_chip[at + occupied : at + 2 * occupied, lanes]
            blocks.append(jnp.where(lane < chips, low, pltpu.roll(high, chips, 1)))
            blocks.append(jnp.where(lane < chips, pltpu.roll(low, chips, 1), high))
        turned = jnp.concatenate(blocks, axis=0).T
        for side in range(2):
            half = turned[side * chips : (side + 1) * chips]
            if part == 0:
                mirror[pl.ds(row + side, chips, stride=4), :] = half
            else:
                mirror[pl.ds(2 * (row + side) + 1, chips, stride=8), :] = half


def combine(part, kept, got, natural_order, chip_order, chips, *before):
    rows, full_virtual = got.shape
    return pl.pallas_call(
        functools.partial(combine_kernel, part=part),
        out_shape=(
            jax.ShapeDtypeStruct((rows, full_virtual), F32),
            jax.ShapeDtypeStruct((chips * (4 + 4 * part), rows), F32),
        ),
        compiler_params=PARAMS,
        cost_estimate=cost(12 * rows * full_virtual * full_virtual, 16 * rows * full_virtual),
        name="combine",
    )(kept, got, natural_order, chip_order, *before)


def subtract_kernel(place, real, imag, mirror, keep, to_core, to_vir, to_both, block):
    vir, core = place[0] % 2, (place[0] // 2) % 2
    here = 2 * block.shape[1]
    rows, full_virtual = real.shape
    occupied = rows // here
    half = full_virtual // 2
    lanes = (slice(0, half), slice(half, full_virtual))
    for part in range(2):
        values = (real, imag)[part][...] - mirror[pl.ds(part, full_virtual, stride=2), :].T
        for row in range(here):
            for side in range(2):
                block[part, row // 2, side, pl.ds(row % 2, occupied, stride=2), :] = values[
                    row * occupied : (row + 1) * occupied, lanes[side]
                ]
    for target, to_side, to_half in (
        (keep, core, vir),
        (to_core, 1 - core, vir),
        (to_vir, core, 1 - vir),
        (to_both, 1 - core, 1 - vir),
    ):
        for part in range(2):
            target[part] = block[part, to_side, to_half].astype(BF16)


def subtract(place, real, imag, mirror):
    rows, full_virtual = real.shape
    piece = jax.ShapeDtypeStruct((2, rows // 2, full_virtual // 2), BF16)
    return pl.pallas_call(
        subtract_kernel,
        out_shape=(piece,) * 4,
        in_specs=[IN_SMEM] + [IN_VMEM] * 3,
        out_specs=(IN_VMEM,) * 4,
        scratch_shapes=[pltpu.VMEM((2, 2, 2, rows // 2, full_virtual // 2), F32)],
        compiler_params=PARAMS,
        name="subtract",
    )(place, real, imag, mirror)


def finish_kernel(place, keep, from_core, from_vir, from_both, out):
    vir, core = place[0] % 2, (place[0] // 2) % 2
    out[:, 2 * core + vir] = keep[...]
    out[:, 2 * (1 - core) + vir] = from_core[...]
    out[:, 2 * core + 1 - vir] = from_vir[...]
    out[:, 2 * (1 - core) + 1 - vir] = from_both[...]


def finish(place, pieces):
    _, rows, width = pieces[0].shape
    return pl.pallas_call(
        finish_kernel,
        out_shape=jax.ShapeDtypeStruct((2, 4, rows, width), BF16),
        in_specs=[IN_SMEM] + [IN_VMEM] * 4,
        out_specs=IN_VMEM,
        compiler_params=PARAMS,
        name="finish",
    )(place, *pieces)


SWAP = [(0, 1), (1, 0)]
SWAP_BOTH = [(0, 3), (1, 2), (2, 1), (3, 0)]


def body(amplitudes, integrals, pair_table, kramers):
    chips = lax.axis_size("chip")
    place = lax.axis_index(("chip", "core", "vir")).astype(jnp.int32).reshape(1)
    windows, summed_occ = integrals.shape[1:3]
    pairs = pair_table.shape[0]
    occupied = pairs // summed_occ
    slots, full_virtual, width = amplitudes.shape[1:]
    here = full_virtual // chips

    pieces = regroup(amplitudes, chips)
    moved = lax.all_to_all(pieces, "chip", split_axis=0, concat_axis=0, tiled=True)
    moved = moved.reshape(-1, width)
    flat = integrals.reshape(2, windows, summed_occ * integrals.shape[3], full_virtual)
    flat = pltpu.with_memory_space_constraint(flat, pltpu.HBM)
    across = lax.ppermute(moved, "core", SWAP)

    tables = pair_table.reshape(chips, 2, slots).transpose(1, 0, 2).reshape(2, 1, chips * slots)
    places = jnp.arange(full_virtual, dtype=jnp.int32)[:, None]
    natural_order = (kramers[None, :] == places).astype(BF16)
    chip_order = (kramers[None, :] == places % chips * here + places // chips).astype(BF16)

    mine, slabs, chooser = order(place, moved, tables, flat, occupied)
    matrices, real, imag = first_window(mine, across, chooser, slabs, occupied)
    got_real = lax.ppermute(real, "vir", SWAP)
    got_imag = lax.ppermute(imag, "vir", SWAP)
    kept = second_window(place, matrices, flat)
    real, before = combine(0, kept, got_real, natural_order, chip_order, chips)
    imag, mirror = combine(1, kept, got_imag, natural_order, chip_order, chips, before)
    mirror = lax.all_to_all(mirror.reshape(chips, 8, -1), "chip", split_axis=0, concat_axis=0, tiled=True)
    keep, to_core, to_vir, to_both = subtract(place, real, imag, mirror.reshape(chips * 8, -1))
    from_vir = lax.ppermute(to_vir, "vir", SWAP)
    from_both = lax.ppermute(to_both, ("core", "vir"), SWAP_BOTH)
    from_core = lax.ppermute(to_core, "core", SWAP)
    got_pieces = (keep, from_core, from_vir, from_both)
    out = finish(place, got_pieces)
    return out.reshape(2, windows, occupied, here // 2, width)


def solution(mesh):
    pair, vir = mesh.devices.shape
    split = Mesh(mesh.devices.reshape(pair // 2, 2, vir), ("chip", "core", "vir"))
    over_pair = ("chip", "core")
    placed = (P(None, over_pair, None, "vir"), P(None, None, None, "vir", None), P(), P())
    return jax.shard_map(
        body,
        mesh=split,
        in_specs=placed,
        out_specs=P(None, None, None, over_pair, "vir"),
        check_vma=False,
    )
```

```python
import functools

import jax
import jax.numpy as jnp
from jax import lax
from jax.experimental import pallas as pl
from jax.experimental.pallas import tpu as pltpu
from jax.sharding import Mesh
from jax.sharding import PartitionSpec as P

F32 = jnp.float32
BF16 = jnp.bfloat16
NT = (((1,), (1,)), ((), ()))
VMEM_LIMIT = 24 * 1024 * 1024
IN_VMEM = pl.BlockSpec(memory_space=pltpu.VMEM)
KS_A_BLOCK = 8
IN_HBM = pl.BlockSpec(memory_space=pl.ANY)
IN_SMEM = pl.BlockSpec(memory_space=pltpu.SMEM)
PARAMS = pltpu.CompilerParams(vmem_limit_bytes=VMEM_LIMIT)


def cost(flops, moved_bytes):
    return pl.CostEstimate(flops=int(flops), bytes_accessed=int(moved_bytes), transcendentals=0)


def regroup_kernel(src, dst, planes, sems):
    parts, slots = src.shape[:2]
    copies = [
        pltpu.make_async_copy(src.at[part, slot], planes.at[part, slot], sems.at[part, slot])
        for part in range(parts)
        for slot in range(slots)
    ]
    for copy in copies:
        copy.start()
    for part in range(parts):
        for slot in range(slots):
            copies[part * slots + slot].wait()
            dst[:, slot * parts + part] = planes[part, slot]


def regroup(amplitudes, chips):
    parts, slots, rows, width = amplitudes.shape
    here = rows // chips
    planes = amplitudes.reshape(parts, slots, chips, here, width)
    return pl.pallas_call(
        regroup_kernel,
        out_shape=jax.ShapeDtypeStruct((chips, parts * slots, here, width), amplitudes.dtype),
        in_specs=[IN_HBM],
        out_specs=IN_VMEM,
        scratch_shapes=[pltpu.VMEM(planes.shape, planes.dtype), pltpu.SemaphoreType.DMA((parts, slots))],
        compiler_params=PARAMS,
        name="regroup",
    )(pltpu.with_memory_space_constraint(planes, pltpu.HBM))


def slab_copies(place, turn, integrals, slabs, sems):
    vir, core = place[0] % 2, (place[0] // 2) % 2
    window = 2 * core + (1 - vir if turn == 0 else vir)
    return [pltpu.make_async_copy(integrals.at[part, window], slabs.at[part], sems.at[part]) for part in range(2)]


def spread_rows(moved, wide, slots_by):
    slots = slots_by.shape[0]
    width = moved.shape[1]
    rows = moved.shape[0] // slots
    pitch = slots + 1
    slots_a_step = 32

    def step(index, carry):
        at = index * slots_a_step
        values = moved[pl.ds(pl.multiple_of(at * rows, slots_a_step * rows), slots_a_step * rows), :].astype(F32)
        for slot in range(slots_a_step):
            wide[pl.ds(at + slot, rows, stride=pitch), :] = values[slot * rows : (slot + 1) * rows]
        return carry

    lax.fori_loop(0, slots // slots_a_step, step, 0)
    for row in range(rows):
        slots_by[:, row * width : (row + 1) * width] = wide[row * pitch : row * pitch + slots, :].astype(BF16)


def order_block(start, chooser, slots_by, matrices, mine, width, occupied):
    ordered = jnp.dot(
        chooser[start * occupied : (start + KS_A_BLOCK) * occupied, :], slots_by[...], preferred_element_type=F32
    ).astype(BF16)
    for k in range(KS_A_BLOCK):
        for row in range(slots_by.shape[1] // width):
            at = slice(row * occupied, (row + 1) * occupied)
            lanes = slice((start + k) * width, (start + k + 1) * width)
            block = ordered[k * occupied : (k + 1) * occupied, row * width : (row + 1) * width]
            matrices[at, lanes] = block if mine is None else mine[at, lanes] + block


def choose(chooser, table, occupied):
    pairs, slots = chooser.shape
    lanes = 128
    row = lax.broadcasted_iota(jnp.int32, (pairs, lanes), 0)
    wanted = row % occupied * (pairs // occupied) + row // occupied
    for start in range(0, slots, lanes):
        chooser[:, start : start + lanes] = (table[:, start : start + lanes] == wanted).astype(BF16)


def order_kernel(place, moved, tables, integrals, matrices, slabs, there, here, wide, slots_by, sems, *, occupied):
    copies = slab_copies(place, 0, integrals, slabs, sems)
    for copy in copies:
        copy.start()
    core = (place[0] // 2) % 2
    choose(here, tables[core], occupied)
    spread_rows(moved, wide, slots_by)
    for start in range(0, here.shape[0] // occupied, KS_A_BLOCK):
        order_block(start, here, slots_by, matrices, None, moved.shape[1], occupied)
    choose(there, tables[1 - core], occupied)
    for copy in copies:
        copy.wait()


def order(place, moved, tables, integrals, occupied):
    slots = tables.shape[2]
    pairs = 2 * slots
    width = moved.shape[1]
    rows = moved.shape[0] // slots
    return pl.pallas_call(
        functools.partial(order_kernel, occupied=occupied),
        out_shape=(
            pltpu.VMEM((rows * occupied, pairs // occupied * width), BF16),
            pltpu.VMEM((2,) + integrals.shape[2:], BF16),
            pltpu.VMEM((pairs, slots), BF16),
        ),
        in_specs=[IN_SMEM, IN_VMEM, IN_VMEM, IN_HBM],
        out_specs=(IN_VMEM,) * 3,
        scratch_shapes=[
            pltpu.VMEM((pairs, slots), BF16),
            pltpu.VMEM(((slots + 1) * rows, width), F32),
            pltpu.VMEM((slots, rows * width), BF16),
            pltpu.SemaphoreType.DMA((2,)),
        ],
        compiler_params=PARAMS,
        cost_estimate=cost(2 * pairs * slots * rows * width, integrals.size),
        name="order",
    )(place, moved, tables, integrals)


def product_into(out, matrices, slabs, copies=()):
    half = matrices.shape[0] // 2
    for copy in copies[:1]:
        copy.wait()
    by_real = jnp.dot(matrices[...], slabs[0], preferred_element_type=F32)
    for copy in copies[1:]:
        copy.wait()
    by_imag = jnp.dot(matrices[...], slabs[1], preferred_element_type=F32)
    out[:half] = by_real[:half] - by_imag[half:]
    out[half:] = by_real[half:] + by_imag[:half]


def first_kernel(mine, moved, chooser, slabs, matrices, out, wide, slots_by, by_real, by_imag, *, occupied):
    half = matrices.shape[0] // 2
    width = moved.shape[1]
    spread_rows(moved, wide, slots_by)
    summed_occ = chooser.shape[0] // occupied
    order_block(0, chooser, slots_by, matrices, mine, width, occupied)
    for start in range(0, summed_occ, KS_A_BLOCK):
        if start + KS_A_BLOCK < summed_occ:
            order_block(start + KS_A_BLOCK, chooser, slots_by, matrices, mine, width, occupied)
        lanes = slice(start * width, (start + KS_A_BLOCK) * width)
        for part, total in enumerate((by_real, by_imag)):
            product = jnp.dot(matrices[:, lanes], slabs[part, lanes], preferred_element_type=F32)
            total[...] = product if start == 0 else total[...] + product
    out[:half] = by_real[:half] - by_imag[half:]
    out[half:] = by_real[half:] + by_imag[:half]


def first_window(mine, moved, chooser, slabs, occupied):
    width = moved.shape[1]
    slots = chooser.shape[1]
    rows = moved.shape[0] // slots
    full_virtual = slabs.shape[-1]
    return pl.pallas_call(
        functools.partial(first_kernel, occupied=occupied),
        out_shape=(
            jax.ShapeDtypeStruct(mine.shape, BF16),
            jax.ShapeDtypeStruct((mine.shape[0], full_virtual), F32),
        ),
        in_specs=[IN_VMEM] * 4,
        out_specs=(IN_VMEM,) * 2,
        scratch_shapes=[
            pltpu.VMEM(((slots + 1) * rows, width), F32),
            pltpu.VMEM((slots, rows * width), BF16),
            pltpu.VMEM((mine.shape[0], full_virtual), F32),
            pltpu.VMEM((mine.shape[0], full_virtual), F32),
        ],
        compiler_params=PARAMS,
        cost_estimate=cost(4 * mine.size * full_virtual, 4 * mine.size),
        name="first_window",
    )(mine, moved, chooser, pltpu.with_memory_space_constraint(slabs, pltpu.VMEM))


def second_kernel(place, matrices, integrals, out, slabs, sems):
    copies = slab_copies(place, 1, integrals, slabs, sems)
    for copy in copies:
        copy.start()
    product_into(out, matrices, slabs, copies)


def second_window(place, matrices, integrals):
    depth, full_virtual = integrals.shape[2:]
    return pl.pallas_call(
        second_kernel,
        out_shape=jax.ShapeDtypeStruct((matrices.shape[0], full_virtual), F32),
        in_specs=[IN_SMEM, IN_VMEM, IN_HBM],
        out_specs=IN_VMEM,
        scratch_shapes=[pltpu.VMEM((2, depth, full_virtual), BF16), pltpu.SemaphoreType.DMA((2,))],
        compiler_params=PARAMS,
        cost_estimate=cost(4 * matrices.size * full_virtual, 4 * matrices.size),
        name="second_window",
    )(place, matrices, integrals)


def chosen(values, orders):
    rows = values.shape[0]
    high = values.astype(BF16)
    rest = values - high.astype(F32)
    middle = rest.astype(BF16)
    low = (rest - middle.astype(F32)).astype(BF16)
    parts = jnp.concatenate([low, middle, high], axis=0)
    parts = lax.dot_general(parts, orders, NT, preferred_element_type=F32)
    return parts[:rows] + parts[rows : 2 * rows] + parts[2 * rows :]


def combine_kernel(kept, got, orders, own, mirror):
    full_virtual = kept.shape[1]
    rows = kept.shape[0] // 2
    chips = mirror.shape[0] // 8
    here = full_virtual // chips
    occupied = rows // here
    lane = lax.broadcasted_iota(jnp.int32, (occupied, 2 * chips), 1)
    values = kept[...] + got[...]
    ordered = chosen(values, orders[...])
    own[...] = ordered[:, :full_virtual]
    by_chip = ordered[:, full_virtual:]
    for part in range(2):
        for row in range(0, here, 2):
            at = part * rows + row * occupied
            blocks = []
            for other in range(0, here, 2):
                lanes = slice(other * chips, (other + 2) * chips)
                low = by_chip[at : at + occupied, lanes]
                high = by_chip[at + occupied : at + 2 * occupied, lanes]
                blocks.append(jnp.where(lane < chips, low, pltpu.roll(high, chips, 1)))
                blocks.append(jnp.where(lane < chips, pltpu.roll(low, chips, 1), high))
            turned = jnp.concatenate(blocks, axis=0).T
            mirror[pl.ds(2 * row + part, chips, stride=8), :] = turned[:chips]
            mirror[pl.ds(2 * (row + 1) + part, chips, stride=8), :] = turned[chips:]


def combine(kept, got, orders, chips):
    return pl.pallas_call(
        combine_kernel,
        out_shape=(jax.ShapeDtypeStruct(kept.shape, F32), jax.ShapeDtypeStruct((chips * 8, kept.shape[0] // 2), F32)),
        compiler_params=PARAMS,
        name="combine",
    )(kept, got, orders)


def subtract_kernel(place, own, mirror, keep, to_core, to_vir, to_both, block):
    vir, core = place[0] % 2, (place[0] // 2) % 2
    here = 2 * block.shape[1]
    rows, full_virtual = own.shape[0] // 2, own.shape[1]
    occupied = rows // here
    half = full_virtual // 2
    lanes = (slice(0, half), slice(half, full_virtual))
    for part in range(2):
        values = own[part * rows : (part + 1) * rows] - mirror[pl.ds(part, full_virtual, stride=2), :].T
        for row in range(here):
            for side in range(2):
                block[part, row // 2, side, pl.ds(row % 2, occupied, stride=2), :] = values[
                    row * occupied : (row + 1) * occupied, lanes[side]
                ]
    for target, to_side, to_half in (
        (keep, core, vir),
        (to_core, 1 - core, vir),
        (to_vir, core, 1 - vir),
        (to_both, 1 - core, 1 - vir),
    ):
        for part in range(2):
            target[part] = block[part, to_side, to_half].astype(BF16)


def subtract(place, own, mirror):
    rows, full_virtual = own.shape[0] // 2, own.shape[1]
    piece = jax.ShapeDtypeStruct((2, rows // 2, full_virtual // 2), BF16)
    return pl.pallas_call(
        subtract_kernel,
        out_shape=(piece,) * 4,
        in_specs=[IN_SMEM, IN_VMEM, IN_VMEM],
        out_specs=(IN_VMEM,) * 4,
        scratch_shapes=[pltpu.VMEM((2, 2, 2, rows // 2, full_virtual // 2), F32)],
        compiler_params=PARAMS,
        name="subtract",
    )(place, own, mirror)


def finish_kernel(place, keep, from_core, from_vir, from_both, out):
    vir, core = place[0] % 2, (place[0] // 2) % 2
    out[:, 2 * core + vir] = keep[...]
    out[:, 2 * (1 - core) + vir] = from_core[...]
    out[:, 2 * core + 1 - vir] = from_vir[...]
    out[:, 2 * (1 - core) + 1 - vir] = from_both[...]


def finish(place, pieces):
    _, rows, width = pieces[0].shape
    return pl.pallas_call(
        finish_kernel,
        out_shape=jax.ShapeDtypeStruct((2, 4, rows, width), BF16),
        in_specs=[IN_SMEM] + [IN_VMEM] * 4,
        out_specs=IN_VMEM,
        compiler_params=PARAMS,
        name="finish",
    )(place, *pieces)


SWAP = [(0, 1), (1, 0)]
SWAP_BOTH = [(0, 3), (1, 2), (2, 1), (3, 0)]


def body(amplitudes, integrals, pair_table, kramers):
    chips = lax.axis_size("chip")
    place = lax.axis_index(("chip", "core", "vir")).astype(jnp.int32).reshape(1)
    windows, summed_occ = integrals.shape[1:3]
    pairs = pair_table.shape[0]
    occupied = pairs // summed_occ
    slots, full_virtual, width = amplitudes.shape[1:]
    here = full_virtual // chips

    pieces = regroup(amplitudes, chips)
    moved = lax.all_to_all(pieces, "chip", split_axis=0, concat_axis=0, tiled=True)
    moved = moved.reshape(-1, width)
    flat = integrals.reshape(2, windows, summed_occ * integrals.shape[3], full_virtual)
    flat = pltpu.with_memory_space_constraint(flat, pltpu.HBM)
    across = lax.ppermute(moved, "core", SWAP)

    tables = pair_table.reshape(chips, 2, slots).transpose(1, 0, 2).reshape(2, 1, chips * slots)
    places = jnp.arange(full_virtual, dtype=jnp.int32)
    places = jnp.concatenate([places, places % chips * here + places // chips])[:, None]
    orders = (kramers[None, :] == places).astype(BF16)

    mine, slabs, chooser = order(place, moved, tables, flat, occupied)
    matrices, to_send = first_window(mine, across, chooser, slabs, occupied)
    got = lax.ppermute(to_send, "vir", SWAP)
    kept = second_window(place, matrices, flat)
    own, mirror = combine(kept, got, orders, chips)
    mirror = lax.all_to_all(mirror.reshape(chips, 8, -1), "chip", split_axis=0, concat_axis=0, tiled=True)
    keep, to_core, to_vir, to_both = subtract(place, own, mirror.reshape(chips * 8, -1))
    from_vir = lax.ppermute(to_vir, "vir", SWAP)
    from_both = lax.ppermute(to_both, ("core", "vir"), SWAP_BOTH)
    from_core = lax.ppermute(to_core, "core", SWAP)
    got_pieces = (keep, from_core, from_vir, from_both)
    out = finish(place, got_pieces)
    return out.reshape(2, windows, occupied, here // 2, width)


def solution(mesh):
    pair, vir = mesh.devices.shape
    split = Mesh(mesh.devices.reshape(pair // 2, 2, vir), ("chip", "core", "vir"))
    over_pair = ("chip", "core")
    placed = (P(None, over_pair, None, "vir"), P(None, None, None, "vir", None), P(), P())
    return jax.shard_map(
        body,
        mesh=split,
        in_specs=placed,
        out_specs=P(None, None, None, over_pair, "vir"),
        check_vma=False,
    )
```

```python
import functools

import jax
import jax.numpy as jnp
from jax import lax
from jax.experimental import pallas as pl
from jax.experimental.pallas import tpu as pltpu
from jax.sharding import Mesh
from jax.sharding import PartitionSpec as P

F32 = jnp.float32
BF16 = jnp.bfloat16
NT = (((1,), (1,)), ((), ()))
VMEM_LIMIT = 24 * 1024 * 1024
IN_VMEM = pl.BlockSpec(memory_space=pltpu.VMEM)
KS_A_BLOCK = 8
IN_HBM = pl.BlockSpec(memory_space=pl.ANY)
IN_SMEM = pl.BlockSpec(memory_space=pltpu.SMEM)
PARAMS = pltpu.CompilerParams(vmem_limit_bytes=VMEM_LIMIT)


def cost(flops, moved_bytes):
    return pl.CostEstimate(flops=int(flops), bytes_accessed=int(moved_bytes), transcendentals=0)


def regroup_kernel(src, dst, planes, sems):
    parts, slots = src.shape[:2]
    copies = [
        pltpu.make_async_copy(src.at[part, slot], planes.at[part, slot], sems.at[part, slot])
        for part in range(parts)
        for slot in range(slots)
    ]
    for copy in copies:
        copy.start()
    for part in range(parts):
        for slot in range(slots):
            copies[part * slots + slot].wait()
            dst[:, slot * parts + part] = planes[part, slot]


def regroup(amplitudes, chips):
    parts, slots, rows, width = amplitudes.shape
    here = rows // chips
    planes = amplitudes.reshape(parts, slots, chips, here, width)
    return pl.pallas_call(
        regroup_kernel,
        out_shape=jax.ShapeDtypeStruct((chips, parts * slots, here, width), amplitudes.dtype),
        in_specs=[IN_HBM],
        out_specs=IN_VMEM,
        scratch_shapes=[pltpu.VMEM(planes.shape, planes.dtype), pltpu.SemaphoreType.DMA((parts, slots))],
        compiler_params=PARAMS,
        name="regroup",
    )(pltpu.with_memory_space_constraint(planes, pltpu.HBM))


def slab_copies(place, turn, integrals, slabs, sems):
    vir, core = place[0] % 2, (place[0] // 2) % 2
    window = 2 * core + (1 - vir if turn == 0 else vir)
    return [pltpu.make_async_copy(integrals.at[part, window], slabs.at[part], sems.at[part]) for part in range(2)]


def spread_rows(moved, wide, slots_by):
    slots = slots_by.shape[0]
    width = moved.shape[1]
    rows = moved.shape[0] // slots
    pitch = slots + 1
    slots_a_step = 32

    def step(index, carry):
        at = index * slots_a_step
        values = moved[pl.ds(pl.multiple_of(at * rows, slots_a_step * rows), slots_a_step * rows), :].astype(F32)
        for slot in range(slots_a_step):
            wide[pl.ds(at + slot, rows, stride=pitch), :] = values[slot * rows : (slot + 1) * rows]
        return carry

    lax.fori_loop(0, slots // slots_a_step, step, 0)
    for row in range(rows):
        slots_by[:, row * width : (row + 1) * width] = wide[row * pitch : row * pitch + slots, :].astype(BF16)


def order_block(start, chooser, slots_by, matrices, mine, width, occupied):
    ordered = jnp.dot(
        chooser[start * occupied : (start + KS_A_BLOCK) * occupied, :], slots_by[...], preferred_element_type=F32
    ).astype(BF16)
    for k in range(KS_A_BLOCK):
        for row in range(slots_by.shape[1] // width):
            at = slice(row * occupied, (row + 1) * occupied)
            lanes = slice((start + k) * width, (start + k + 1) * width)
            block = ordered[k * occupied : (k + 1) * occupied, row * width : (row + 1) * width]
            matrices[at, lanes] = block if mine is None else mine[at, lanes] + block


def choose(chooser, table, occupied):
    pairs, slots = chooser.shape
    lanes = 128
    row = lax.broadcasted_iota(jnp.int32, (pairs, lanes), 0)
    wanted = row % occupied * (pairs // occupied) + row // occupied
    for start in range(0, slots, lanes):
        chooser[:, start : start + lanes] = (table[:, start : start + lanes] == wanted).astype(BF16)


def order_kernel(place, moved, tables, integrals, matrices, slabs, there, here, wide, slots_by, sems, *, occupied):
    copies = slab_copies(place, 0, integrals, slabs, sems)
    for copy in copies:
        copy.start()
    core = (place[0] // 2) % 2
    choose(here, tables[core], occupied)
    spread_rows(moved, wide, slots_by)
    for start in range(0, here.shape[0] // occupied, KS_A_BLOCK):
        order_block(start, here, slots_by, matrices, None, moved.shape[1], occupied)
    choose(there, tables[1 - core], occupied)
    for copy in copies:
        copy.wait()


def order(place, moved, tables, integrals, occupied):
    slots = tables.shape[2]
    pairs = 2 * slots
    width = moved.shape[1]
    rows = moved.shape[0] // slots
    return pl.pallas_call(
        functools.partial(order_kernel, occupied=occupied),
        out_shape=(
            pltpu.VMEM((rows * occupied, pairs // occupied * width), BF16),
            pltpu.VMEM((2,) + integrals.shape[2:], BF16),
            pltpu.VMEM((pairs, slots), BF16),
        ),
        in_specs=[IN_SMEM, IN_VMEM, IN_VMEM, IN_HBM],
        out_specs=(IN_VMEM,) * 3,
        scratch_shapes=[
            pltpu.VMEM((pairs, slots), BF16),
            pltpu.VMEM(((slots + 1) * rows, width), F32),
            pltpu.VMEM((slots, rows * width), BF16),
            pltpu.SemaphoreType.DMA((2,)),
        ],
        compiler_params=PARAMS,
        cost_estimate=cost(2 * pairs * slots * rows * width, integrals.size),
        name="order",
    )(place, moved, tables, integrals)


def product_into(out, matrices, slabs, copies=()):
    half = matrices.shape[0] // 2
    for copy in copies[:1]:
        copy.wait()
    by_real = jnp.dot(matrices[...], slabs[0], preferred_element_type=F32)
    for copy in copies[1:]:
        copy.wait()
    by_imag = jnp.dot(matrices[...], slabs[1], preferred_element_type=F32)
    out[:half] = by_real[:half] - by_imag[half:]
    out[half:] = by_real[half:] + by_imag[:half]


def first_kernel(mine, moved, chooser, slabs, matrices, out, wide, slots_by, by_real, by_imag, *, occupied):
    half = matrices.shape[0] // 2
    width = moved.shape[1]
    spread_rows(moved, wide, slots_by)
    summed_occ = chooser.shape[0] // occupied
    order_block(0, chooser, slots_by, matrices, mine, width, occupied)
    for start in range(0, summed_occ, KS_A_BLOCK):
        if start + KS_A_BLOCK < summed_occ:
            order_block(start + KS_A_BLOCK, chooser, slots_by, matrices, mine, width, occupied)
        lanes = slice(start * width, (start + KS_A_BLOCK) * width)
        for part, total in enumerate((by_real, by_imag)):
            product = jnp.dot(matrices[:, lanes], slabs[part, lanes], preferred_element_type=F32)
            total[...] = product if start == 0 else total[...] + product
    out[:half] = by_real[:half] - by_imag[half:]
    out[half:] = by_real[half:] + by_imag[:half]


def first_window(mine, moved, chooser, slabs, occupied):
    width = moved.shape[1]
    slots = chooser.shape[1]
    rows = moved.shape[0] // slots
    full_virtual = slabs.shape[-1]
    return pl.pallas_call(
        functools.partial(first_kernel, occupied=occupied),
        out_shape=(
            jax.ShapeDtypeStruct(mine.shape, BF16),
            jax.ShapeDtypeStruct((mine.shape[0], full_virtual), F32),
        ),
        in_specs=[IN_VMEM] * 4,
        out_specs=(IN_VMEM,) * 2,
        scratch_shapes=[
            pltpu.VMEM(((slots + 1) * rows, width), F32),
            pltpu.VMEM((slots, rows * width), BF16),
            pltpu.VMEM((mine.shape[0], full_virtual), F32),
            pltpu.VMEM((mine.shape[0], full_virtual), F32),
        ],
        compiler_params=PARAMS,
        cost_estimate=cost(4 * mine.size * full_virtual, 4 * mine.size),
        name="first_window",
    )(mine, moved, chooser, pltpu.with_memory_space_constraint(slabs, pltpu.VMEM))


def second_kernel(place, matrices, integrals, out, slabs, sems):
    copies = slab_copies(place, 1, integrals, slabs, sems)
    for copy in copies:
        copy.start()
    product_into(out, matrices, slabs, copies)


def second_window(place, matrices, integrals):
    depth, full_virtual = integrals.shape[2:]
    return pl.pallas_call(
        second_kernel,
        out_shape=jax.ShapeDtypeStruct((matrices.shape[0], full_virtual), F32),
        in_specs=[IN_SMEM, IN_VMEM, IN_HBM],
        out_specs=IN_VMEM,
        scratch_shapes=[pltpu.VMEM((2, depth, full_virtual), BF16), pltpu.SemaphoreType.DMA((2,))],
        compiler_params=PARAMS,
        cost_estimate=cost(4 * matrices.size * full_virtual, 4 * matrices.size),
        name="second_window",
    )(place, matrices, integrals)


def chosen(values, order_by):
    high = values.astype(BF16)
    rest = values - high.astype(F32)
    middle = rest.astype(BF16)
    low = (rest - middle.astype(F32)).astype(BF16)
    total = lax.dot_general(low, order_by, NT, preferred_element_type=F32)
    total += lax.dot_general(middle, order_by, NT, preferred_element_type=F32)
    return total + lax.dot_general(high, order_by, NT, preferred_element_type=F32)


def combine_kernel(kept, got, natural_order, chip_order, own, mirror):
    full_virtual = kept.shape[1]
    rows = kept.shape[0] // 2
    chips = mirror.shape[0] // 8
    here = full_virtual // chips
    occupied = rows // here
    lane = lax.broadcasted_iota(jnp.int32, (occupied, 2 * chips), 1)
    values = kept[...] + got[...]
    by_chip = chosen(values, chip_order[...])
    own[...] = chosen(values, natural_order[...])
    for part in range(2):
        for row in range(0, here, 2):
            at = part * rows + row * occupied
            blocks = []
            for other in range(0, here, 2):
                lanes = slice(other * chips, (other + 2) * chips)
                low = by_chip[at : at + occupied, lanes]
                high = by_chip[at + occupied : at + 2 * occupied, lanes]
                blocks.append(jnp.where(lane < chips, low, pltpu.roll(high, chips, 1)))
                blocks.append(jnp.where(lane < chips, pltpu.roll(low, chips, 1), high))
            turned = jnp.concatenate(blocks, axis=0).T
            mirror[pl.ds(2 * row + part, chips, stride=8), :] = turned[:chips]
            mirror[pl.ds(2 * (row + 1) + part, chips, stride=8), :] = turned[chips:]


def combine(kept, got, natural_order, chip_order, chips):
    return pl.pallas_call(
        combine_kernel,
        out_shape=(jax.ShapeDtypeStruct(kept.shape, F32), jax.ShapeDtypeStruct((chips * 8, kept.shape[0] // 2), F32)),
        in_specs=[IN_VMEM] * 4,
        out_specs=(IN_VMEM,) * 2,
        compiler_params=PARAMS,
        name="combine",
    )(kept, got, natural_order, chip_order)


def subtract_kernel(place, own, mirror, keep, to_core, to_vir, to_both, block):
    vir, core = place[0] % 2, (place[0] // 2) % 2
    here = 2 * block.shape[1]
    rows, full_virtual = own.shape[0] // 2, own.shape[1]
    occupied = rows // here
    half = full_virtual // 2
    lanes = (slice(0, half), slice(half, full_virtual))
    for part in range(2):
        values = own[part * rows : (part + 1) * rows] - mirror[pl.ds(part, full_virtual, stride=2), :].T
        for row in range(here):
            for side in range(2):
                block[part, row // 2, side, pl.ds(row % 2, occupied, stride=2), :] = values[
                    row * occupied : (row + 1) * occupied, lanes[side]
                ]
    for target, to_side, to_half in (
        (keep, core, vir),
        (to_core, 1 - core, vir),
        (to_vir, core, 1 - vir),
        (to_both, 1 - core, 1 - vir),
    ):
        for part in range(2):
            target[part] = block[part, to_side, to_half].astype(BF16)


def subtract(place, own, mirror):
    rows, full_virtual = own.shape[0] // 2, own.shape[1]
    piece = jax.ShapeDtypeStruct((2, rows // 2, full_virtual // 2), BF16)
    return pl.pallas_call(
        subtract_kernel,
        out_shape=(piece,) * 4,
        in_specs=[IN_SMEM, IN_VMEM, IN_VMEM],
        out_specs=(IN_VMEM,) * 4,
        scratch_shapes=[pltpu.VMEM((2, 2, 2, rows // 2, full_virtual // 2), F32)],
        compiler_params=PARAMS,
        name="subtract",
    )(place, own, mirror)


def finish_kernel(place, keep, from_core, from_vir, from_both, out):
    vir, core = place[0] % 2, (place[0] // 2) % 2
    out[:, 2 * core + vir] = keep[...]
    out[:, 2 * (1 - core) + vir] = from_core[...]
    out[:, 2 * core + 1 - vir] = from_vir[...]
    out[:, 2 * (1 - core) + 1 - vir] = from_both[...]


def finish(place, pieces):
    _, rows, width = pieces[0].shape
    return pl.pallas_call(
        finish_kernel,
        out_shape=jax.ShapeDtypeStruct((2, 4, rows, width), BF16),
        in_specs=[IN_SMEM] + [IN_VMEM] * 4,
        out_specs=IN_VMEM,
        compiler_params=PARAMS,
        name="finish",
    )(place, *pieces)


SWAP = [(0, 1), (1, 0)]
SWAP_BOTH = [(0, 3), (1, 2), (2, 1), (3, 0)]


def body(amplitudes, integrals, pair_table, kramers):
    chips = lax.axis_size("chip")
    place = lax.axis_index(("chip", "core", "vir")).astype(jnp.int32).reshape(1)
    windows, summed_occ = integrals.shape[1:3]
    pairs = pair_table.shape[0]
    occupied = pairs // summed_occ
    slots, full_virtual, width = amplitudes.shape[1:]
    here = full_virtual // chips

    pieces = regroup(amplitudes, chips)
    moved = lax.all_to_all(pieces, "chip", split_axis=0, concat_axis=0, tiled=True)
    moved = moved.reshape(-1, width)
    flat = integrals.reshape(2, windows, summed_occ * integrals.shape[3], full_virtual)
    flat = pltpu.with_memory_space_constraint(flat, pltpu.HBM)
    across = lax.ppermute(moved, "core", SWAP)

    tables = pair_table.reshape(chips, 2, slots).transpose(1, 0, 2).reshape(2, 1, chips * slots)
    places = jnp.arange(full_virtual, dtype=jnp.int32)[:, None]
    natural_order = (kramers[None, :] == places).astype(BF16)
    chip_order = (kramers[None, :] == places % chips * here + places // chips).astype(BF16)

    mine, slabs, chooser = order(place, moved, tables, flat, occupied)
    matrices, to_send = first_window(mine, across, chooser, slabs, occupied)
    got = lax.ppermute(to_send, "vir", SWAP)
    kept = second_window(place, matrices, flat)
    own, mirror = combine(kept, got, natural_order, chip_order, chips)
    mirror = lax.all_to_all(mirror.reshape(chips, 8, -1), "chip", split_axis=0, concat_axis=0, tiled=True)
    keep, to_core, to_vir, to_both = subtract(place, own, mirror.reshape(chips * 8, -1))
    from_vir = lax.ppermute(to_vir, "vir", SWAP)
    from_both = lax.ppermute(to_both, ("core", "vir"), SWAP_BOTH)
    from_core = lax.ppermute(to_core, "core", SWAP)
    got_pieces = (keep, from_core, from_vir, from_both)
    out = finish(place, got_pieces)
    return out.reshape(2, windows, occupied, here // 2, width)


def solution(mesh):
    pair, vir = mesh.devices.shape
    split = Mesh(mesh.devices.reshape(pair // 2, 2, vir), ("chip", "core", "vir"))
    over_pair = ("chip", "core")
    placed = (P(None, over_pair, None, "vir"), P(None, None, None, "vir", None), P(), P())
    return jax.shard_map(
        body,
        mesh=split,
        in_specs=placed,
        out_specs=P(None, None, None, over_pair, "vir"),
        check_vma=False,
    )
```
